256 devices in a mesh: ta: 16 (over y, x), gz: 8 (over z_hi, core), gy: 2 (over z_lo).
Axes of the slice: x: 4, y: 4, z: 8 (z_hi: 4, z_lo: 2; z = z_hi * 2 + z_lo), core: 2. Of those that a mesh axis runs over, the one named last changes fastest.
Arguments:
- current: float32 [96, 48, 2304], P('ta', 'gz', 'gy'), may hold values from -12 to 12
- kernel: float32 [96, 96, 18432], P('ta', 'gz', 'gy'), as said below
Outputs:
- potential: float32 [96, 48, 2304], P('ta', 'gz', 'gy')
The draws below stay inside these ranges and needn't reach their ends.
Inputs may be any that keep to these rules, and one draw needn't show every extreme that they name: kernel is zero at the zero momentum (all four indices 0) and positive at every other momentum.
All inputs are finite; a program needn't handle non-finite values.
Results may differ from the reference program's by a relative error of at most 0.018.
Values may be sent and summed in bfloat16 or wider, within the bound.
No kernel may reach another device: no remote copies, remote signals or barrier semaphores. Data moves between devices by JAX's collectives and lax.ppermute only.
A program may use at most 64 MiB of HBM per device.

```python
import math
import jax
import jax.numpy as jnp
from jax import lax

LX = 48
LY = 48
LZ = 48
LT = 96


def draw_current(key, part):
    key = jax.random.fold_in(key, 11)
    values = jnp.clip(2.0 * jax.random.normal(key, (LT, LZ, LY * LX), jnp.float32), -12.0, 12.0)
    return values


def lattice_term(position, period):
    angles = position.astype(jnp.float32) * (math.pi / period)
    return 4.0 * jnp.sin(angles) ** 2


def draw_kernel(key, part):
    key = jax.random.fold_in(key, 23)
    shape = (2 * LZ, 2 * LY, 2 * LX, 2 * LT)
    third = lax.broadcasted_iota(jnp.int32, shape, 0)
    second = lax.broadcasted_iota(jnp.int32, shape, 1)
    first = lax.broadcasted_iota(jnp.int32, shape, 2)
    timing = lax.broadcasted_iota(jnp.int32, shape, 3)
    momentum = lattice_term(third, 2 * LZ) + lattice_term(second, 2 * LY)
    momentum = momentum + lattice_term(first, 2 * LX) + lattice_term(timing, 2 * LT)
    anchor = (third + second + first + timing == 0).astype(jnp.float32)
    factor = jax.random.uniform(key, shape, jnp.float32, 0.5, 1.5)
    values = factor * (1.0 - anchor) / (momentum + anchor)
    return values.reshape(2 * LZ, 2 * LY, 2 * LX * 2 * LT)


def setup_inputs(seed: int = 0) -> dict:
    key_list = jax.random.split(jax.random.key(seed), 3)
    return {
        "current": draw_current(jax.random.fold_in(key_list[2], 71), 0),
        "kernel": draw_kernel(jax.random.fold_in(key_list[2], 71), 0),
    }


def rounded(values):
    real_part = lax.optimization_barrier(jnp.real(values).astype(jnp.bfloat16)).astype(jnp.float32)
    imag_part = lax.optimization_barrier(jnp.imag(values).astype(jnp.bfloat16)).astype(jnp.float32)
    return lax.complex(real_part, imag_part)


def reference(current, kernel):
    kernel = kernel.reshape(2 * LZ, 2 * LY, 2 * LX, 2 * LT)
    field = current.reshape(LT, LZ, LY, LX)
    spectrum = rounded(jnp.fft.fft(field, n=2 * LX, axis=3))
    spectrum = rounded(jnp.fft.fft(spectrum, n=2 * LY, axis=2))
    spectrum = rounded(jnp.fft.fft(spectrum, n=2 * LZ, axis=1))

    def slab_turn(position):
        layer_data = lax.dynamic_index_in_dim(spectrum, position, axis=1, keepdims=False)
        weights = jnp.moveaxis(lax.dynamic_index_in_dim(kernel, position, axis=0, keepdims=False), 2, 0)
        product = jnp.fft.fft(layer_data, n=2 * LT, axis=0) * weights
        inverse = jnp.fft.ifft(product, axis=0)[:LT]
        return rounded(inverse)

    slabs = lax.map(slab_turn, jnp.arange(2 * LZ, dtype=jnp.int32))
    slabs = rounded(jnp.fft.ifft(slabs, axis=0)[:LZ])
    slabs = rounded(jnp.fft.ifft(slabs, axis=2)[:, :, :LY])
    result = jnp.real(jnp.fft.ifft(slabs, axis=3))[..., :LX]
    return jnp.moveaxis(result, 0, 1).reshape(LT, LZ, LY * LX)
```

```python
import numpy as np

import jax
import jax.numpy as jnp
from jax import lax
from jax.experimental import pallas as pl
from jax.experimental.pallas import tpu as pltpu
from jax.sharding import PartitionSpec as P


BF = jnp.bfloat16
F32 = jnp.float32
AXES = ("ta", "gz", "gy")
PARTS = (2, 3)
SHIFTS = (0, 1, 7, 2, 6, 3, 5, 4)


def split_table(table):
    table = np.asarray(table, np.float32)
    upper = table.astype(jnp.bfloat16)
    lower = (table - upper.astype(np.float32)).astype(jnp.bfloat16)
    return np.stack([upper, lower])


def turn(numerator, period, sign):
    angle = 2.0 * np.pi * (np.asarray(numerator) % period) / period
    cosine, sine = np.cos(angle), sign * np.sin(angle)
    return np.stack([np.stack([cosine, -sine]), np.stack([sine, cosine])])


def first_forward():
    x = np.arange(48)
    i = np.arange(25)
    parts = turn(x[:, None] * i[None, :], 96, -1.0)[:, 0]
    table = np.zeros((8, 48, 5, 128))
    for y in range(8):
        block = parts.reshape(2, 48, 5, 5).transpose(1, 2, 0, 3).reshape(48, 5, 10)
        table[y, :, :, y * 10 : y * 10 + 10] = block
    return split_table(table.reshape(384, 640))


def second_forward():
    y = np.arange(48)
    out = np.zeros((8, 6, 128, 2, 64))
    for g in range(8):
        q = 12 * g + np.arange(12)
        parts = turn(y[:, None] * q[None, :], 96, -1.0)
        for i in range(5):
            for inp in range(2):
                for r in range(8):
                    out[g, :, r * 10 + inp * 5 + i, :, i * 12 : i * 12 + 12] = parts[
                        :, inp, r::8
                    ].transpose(1, 0, 2)
    table = split_table(out.reshape(8, 768, 128))
    return np.concatenate([table[0], table[1]], axis=2)


def third_forward():
    w = np.arange(96)
    z = np.arange(48)
    parts = turn(w[:, None] * z[None, :], 96, -1.0)
    table = np.zeros((96, 2, 2, 8, 8))
    table[..., :6] = parts.transpose(2, 0, 1, 3).reshape(96, 2, 2, 8, 6)
    return split_table(table.reshape(192, 128))


def time_forward():
    k = np.arange(192)
    t = np.arange(96)
    parts = turn(k[:, None] * t[None, :], 192, -1.0)
    parts = parts.transpose(0, 2, 3, 1).reshape(2, 192, 16, 6, 2).transpose(0, 1, 2, 4, 3)
    table = np.zeros((4, 2, 192, 16, 2, 8))
    table[0, ..., :6] = parts
    for s in range(3):
        table[1 + s, ..., 6:8] = parts[..., 2 * s : 2 * s + 2]
    return split_table(table.reshape(4, 384, 256))


def time_inverse():
    k = np.arange(192)
    t = np.arange(96)
    parts = turn(t[:, None] * k[None, :], 192, 1.0) / 192.0
    parts = parts.reshape(2, 2, 16, 6, 192).transpose(2, 0, 3, 1, 4)
    table = np.zeros((4, 16, 2, 8, 2, 192))
    table[0, :, :, :6] = parts
    for s in range(3):
        table[1 + s, :, :, 6:8] = parts[:, :, 2 * s : 2 * s + 2]
    return split_table(table.reshape(4, 256, 384))


def third_inverse():
    w = np.arange(96)
    z = np.arange(48)
    parts = turn(z[:, None] * w[None, :], 96, 1.0) / 96.0
    parts = parts.reshape(2, 2, 8, 6, 96).transpose(2, 0, 3, 4, 1)
    table = np.zeros((4, 8, 2, 8, 96, 2))
    table[0, :, :, :6] = parts
    for s in range(3):
        table[1 + s, :, :, 6:8] = parts[:, :, 2 * s : 2 * s + 2]
    return split_table(table.reshape(4, 128, 192))


def second_inverse():
    q = np.arange(96)
    y = np.arange(48)
    parts = turn(q[:, None] * y[None, :], 96, 1.0) / 96.0
    parts = parts.reshape(2, 2, 8, 12, 6, 8)
    table = np.zeros((8, 2, 64, 6, 128))
    for i in range(5):
        for r in range(8):
            for out in range(2):
                table[:, :, i * 12 : i * 12 + 12, :, r * 10 + out * 5 + i] = parts[
                    out, :, :, :, :, r
                ].transpose(1, 0, 2, 3)
    return split_table(table.reshape(1024, 768))


def first_inverse():
    i = np.arange(25)
    x = np.arange(48)
    parts = turn(i[:, None] * x[None, :], 96, 1.0)[0] / 96.0
    table = np.zeros((5, 128, 8, 48))
    for r in range(8):
        for inp in range(2):
            table[:, r * 10 + inp * 5 : r * 10 + inp * 5 + 5, r] = parts[inp].reshape(5, 5, 48)
    return split_table(table.reshape(640, 384))


def mirror_tables():
    flip = np.zeros((192, 192))
    flip[np.arange(192), (-np.arange(192)) % 192] = 1.0
    order = np.zeros((256, 256))
    for group in range(4):
        for i in range(5):
            for q in range(12):
                row = group * 64 + i * 12
                order[row + q, row + (12 - q) % 12] = 1.0
    return flip.astype(jnp.bfloat16), order.astype(jnp.bfloat16), np.eye(192).astype(jnp.bfloat16)


def dot(left, right):
    return lax.dot_general(left, right, (((1,), (0,)), ((), ())), preferred_element_type=F32)


def dot_rows(left, right):
    return lax.dot_general(left, right, (((1,), (1,)), ((), ())), preferred_element_type=F32)


def low_half(shape):
    return lax.broadcasted_iota(jnp.int32, shape, 1) % 128 < 64


def swap_half(values):
    return pltpu.roll(values, 64, 1)


def call(kernel, out_shape, scratch=(), in_specs=None, grid=(), vmem=14, flops=10**8, moved=4 * 10**6):
    placed = {} if in_specs is None else {"in_specs": in_specs}
    return pl.pallas_call(
        kernel,
        out_shape=out_shape,
        **placed,
        grid=grid,
        scratch_shapes=list(scratch),
        compiler_params=pltpu.CompilerParams(vmem_limit_bytes=vmem * 2**20),
        cost_estimate=pl.CostEstimate(flops=flops, bytes_accessed=moved, transcendentals=0),
    )


def vmem_spec():
    return pl.BlockSpec(memory_space=pltpu.VMEM)


def smem_spec():
    return pl.BlockSpec(memory_space=pltpu.SMEM)


def raw_kernel(current_ref, out_ref, work):
    work[...] = jnp.zeros_like(work)
    for t in range(6):
        work[8 * t : 8 * t + 6, :] = current_ref[t]
    out_ref[...] = work[...].astype(BF)


def part_of(plane):
    for part, count in enumerate(PARTS):
        if plane < count:
            return part, plane
        plane -= count


def weight_send_kernel(kernel_ref, *refs):
    plane_ref, line_ref, corner_ref, work, rows = refs[len(PARTS) :]
    rows[...] = jnp.zeros_like(rows)
    for w in range(6):
        for c in range(4):
            piece = kernel_ref[w, :, 1152 * c : 1152 * (c + 1)]
            work[12 * c : 12 * c + 12, :] = piece
            rows[4 * w + c : 4 * w + c + 1, :] = piece[0:1]
        if w == 0:
            plane_ref[...] = work[...].astype(BF)
        else:
            part, place = part_of(w - 1)
            refs[part][place] = work[...].astype(BF)
    line_ref[...] = rows[4:36, :].astype(BF)
    corner_ref[...] = rows[0:16, :].astype(BF)


def weight_own_kernel(kernel_ref, eye_ref, out_ref, work):
    eye = eye_ref[...]
    work[...] = jnp.zeros_like(work)
    for w in range(6):
        for i in range(25):
            piece = kernel_ref[w, :, 192 * i : 192 * (i + 1)]
            row = 64 * (i // 5) + 12 * (i % 5)
            if i < 20:
                work[w, row : row + 12, :] = piece
            else:
                row = 64 * (w // 2) + 12 * (i % 5)
                work[6 + w % 2, row : row + 12, :] = piece
    for v in range(8):
        values = work[v]
        upper = values.astype(BF)
        lower = (values - upper.astype(F32)).astype(BF)
        out_ref[v] = dot_rows(eye, upper) + dot_rows(eye, lower)


def weight_pair_kernel(own_ref, *refs):
    plane_ref, line_ref, corner_ref, flip_ref, order_ref, out_ref, work, held, rows = refs[
        len(PARTS) :
    ]
    flip, order = flip_ref[...], order_ref[...]
    work[...] = jnp.zeros_like(work)
    rows[0:16, :] = corner_ref[...].astype(F32)
    rows[16:48, :] = line_ref[...].astype(F32)
    for w in range(6):
        if w == 0:
            held[...] = plane_ref[...].astype(F32)
            first = 0
        else:
            part, place = part_of(5 - w)
            held[...] = refs[part][place].astype(F32)
            first = 16 + 4 * (5 - w)
        for i in range(1, 24):
            c, p = (24 - i) // 6, (24 - i) % 6
            piece = held[12 * c : 12 * c + 12, 192 * p : 192 * (p + 1)]
            line = rows[first + c : first + c + 1, 192 * p : 192 * (p + 1)]
            if i < 20:
                v, row = w, 64 * (i // 5) + 12 * (i % 5)
            else:
                v, row = 6 + w % 2, 64 * (w // 2) + 12 * (i % 5)
            work[v, row : row + 12, :] = piece
            work[v, row : row + 1, :] = line
    for v in range(8):
        turned = dot(order, work[v].astype(BF)).astype(BF)
        out_ref[v] = own_ref[v] + dot_rows(flip, turned)


def put_rows(work, row, count, values):
    work[0, pl.ds(row, count, stride=8), :] = values[:, :128]
    work[1, pl.ds(row, count, stride=8), :] = values[:, 128:]


def get_rows(work, row, count):
    halves = [work[n, pl.ds(row, count, stride=8), :] for n in range(2)]
    return jnp.concatenate(halves, axis=1)


def forward_kernel(info_ref, *refs):
    blocks = refs[:16]
    ta_ref, tb_ref, t3_ref, out_ref, raw, half, work = refs[16:]
    place, core = info_ref[0], info_ref[1]
    for n in range(16):
        spot = lax.rem(place + SHIFTS[n // 2], 8)
        side = lax.rem(spot, 2)
        plane = (spot // 2) * 2 + (core if n % 2 == 0 else 1 - core)
        for y in range(3):
            raw[side * 3 + y, plane] = blocks[n][:, 384 * y : 384 * (y + 1)]
    for y in range(6):
        rows = raw[y].reshape(384, 384)
        half[y] = (dot(rows, ta_ref[0]) + dot(rows, ta_ref[1])).astype(BF)
    seconds = []
    for ig in range(5):
        merged = jnp.concatenate([half[y, :, 128 * ig : 128 * (ig + 1)] for y in range(6)], axis=1)
        both = dot(merged, tb_ref[...])
        seconds.append(both[:, :128] + both[:, 128:])
    low = low_half((384, 128))
    real_main, imag_main = [], []
    for pair in range(2):
        left, right = seconds[2 * pair], seconds[2 * pair + 1]
        real_main.append(jnp.where(low, left, swap_half(right)))
        imag_main.append(jnp.where(low, swap_half(left), right))
    real_main = jnp.concatenate(real_main, axis=1).reshape(8, 6, 8, 256)
    imag_main = jnp.concatenate(imag_main, axis=1).reshape(8, 6, 8, 256)
    last = seconds[4].reshape(8, 6, 8, 128)
    turned = swap_half(seconds[4]).reshape(8, 6, 8, 128)
    low = low_half((64, 128))

    def finish(row, real_part, imag_part):
        merged = jnp.concatenate([real_part, imag_part], axis=0).astype(BF)
        put_rows(work, row, 192, dot(t3_ref[0], merged) + dot(t3_ref[1], merged))

    for t in range(6):
        finish(t, real_main[:, t].reshape(64, 256), imag_main[:, t].reshape(64, 256))
    for e in range(2):
        plain = [last[:, e + 2 * s].reshape(64, 128) for s in range(3)]
        moved = [turned[:, e + 2 * s].reshape(64, 128) for s in range(3)]
        real_part = [jnp.where(low, plain[0], moved[1]), jnp.where(low, plain[2], 0.0)]
        imag_part = [jnp.where(low, moved[0], plain[1]), jnp.where(low, moved[2], 0.0)]
        finish(6 + e, jnp.concatenate(real_part, axis=1), jnp.concatenate(imag_part, axis=1))
    merged = jnp.concatenate([work[0], work[1]], axis=1)
    out_ref[...] = merged.reshape(16, 6, 16, 256).astype(BF)


def gather_groups(pieces):
    pieces = pieces + [jnp.zeros_like(pieces[0])]
    return jnp.concatenate(pieces, axis=1)


def time_kernel(in_ref, weight_ref, forward_ref, inverse_ref, out_ref):
    def weighted(values, v):
        weight = weight_ref[v]
        return (values * jnp.concatenate([weight, weight], axis=0)).astype(BF)

    def forward(rows, n):
        return dot(forward_ref[0, n], rows) + dot(forward_ref[1, n], rows)

    def inverse(rows, n):
        return dot(inverse_ref[0, n], rows) + dot(inverse_ref[1, n], rows)

    loaded = [in_ref[:, w].reshape(256, 256) for w in range(6)]
    for e in range(2):
        total = None
        for s in range(3):
            rows = gather_groups([loaded[2 * r + e][:, 64 * s : 64 * (s + 1)] for r in range(3)])
            term = forward(rows, 1 + s)
            total = term if total is None else total + term
        spectrum = weighted(total, 6 + e)
        tails = [inverse(spectrum, 1 + s) for s in range(3)]
        for r in range(3):
            w = 2 * r + e
            values = inverse(weighted(forward(loaded[w], 0), w), 0)
            values = values + gather_groups([tail[:, 64 * r : 64 * (r + 1)] for tail in tails])
            out_ref[:, w] = values.astype(BF).reshape(16, 16, 256)


def third_kernel(in_ref, table_ref, out_ref, work):
    values = in_ref[...].astype(F32).reshape(1536, 256)
    work[0] = values[:, :128]
    work[1] = values[:, 128:]

    def inverse(rows, n):
        return dot(table_ref[0, n], rows) + dot(table_ref[1, n], rows)

    def load(row):
        return get_rows(work, row, 192).astype(BF)

    for e in range(2):
        rows = load(6 + e)
        tails = [inverse(rows, 1 + s) for s in range(3)]
        for r in range(3):
            t = 2 * r + e
            values = inverse(load(t), 0)
            values = values + gather_groups([tail[:, 64 * r : 64 * (r + 1)] for tail in tails])
            out_ref[:, t] = values.astype(BF).reshape(8, 16, 256)


def last_kernel(info_ref, in_ref, tb_ref, ta_ref, sign_ref, own_ref, send_ref, work, spare, both):
    side = info_ref[2]
    values = in_ref[...].astype(F32).reshape(768, 256)
    work[0] = values[:, :128]
    work[1] = values[:, 128:]
    spare[...] = jnp.zeros_like(spare)
    for e in range(2):
        rows = get_rows(work, 6 + e, 96)
        spare[pl.ds(e, 96, stride=8), :] = rows[:, :128]
        spare[pl.ds(2 + e, 96, stride=8), :] = swap_half(rows[:, :128])
        spare[pl.ds(4 + e, 96, stride=8), :] = rows[:, 128:]
    low = low_half((48, 128))
    groups = [[] for _ in range(5)]
    shaped = values.reshape(8, 6, 2, 8, 256)
    shaped_spare = spare[...].reshape(8, 6, 2, 8, 128)
    for g in range(8):
        real_part = shaped[g, :, 0].reshape(48, 256)
        imag_part = shaped[g, :, 1].reshape(48, 256)
        for pair in range(2):
            real_tile = real_part[:, 128 * pair : 128 * (pair + 1)]
            imag_tile = imag_part[:, 128 * pair : 128 * (pair + 1)]
            groups[2 * pair].append(jnp.where(low, real_tile, swap_half(imag_tile)))
            groups[2 * pair + 1].append(jnp.where(low, swap_half(real_tile), imag_tile))
        real_tile = shaped_spare[g, :, 0].reshape(48, 128)
        imag_tile = shaped_spare[g, :, 1].reshape(48, 128)
        groups[4].append(jnp.where(low, real_tile, swap_half(imag_tile)))
    rows = jnp.concatenate([jnp.concatenate(group, axis=1) for group in groups], axis=0).astype(BF)
    half = (dot(rows, tb_ref[0]) + dot(rows, tb_ref[1])).astype(BF)
    rows = jnp.concatenate(
        [
            jnp.concatenate(
                [half[48 * ig : 48 * (ig + 1), 128 * y : 128 * (y + 1)] for ig in range(5)], axis=1
            )
            for y in range(6)
        ],
        axis=0,
    )
    result = (dot(rows, ta_ref[0]) + dot(rows, ta_ref[1])) * sign_ref[...]
    for y in range(6):
        both[y // 3, :, 384 * (y % 3) : 384 * (y % 3 + 1)] = result[48 * y : 48 * (y + 1)]
    own = both[side]
    for t in range(6):
        own_ref[t] = own[8 * t : 8 * t + 6]
    send_ref[...] = both[1 - side].astype(BF)


def sum_kernel(own_ref, other_ref, out_ref):
    other = other_ref[...].astype(F32)
    for t in range(6):
        out_ref[t] = own_ref[t] + other[8 * t : 8 * t + 6]


def device_of(a, z, c):
    return (a * 8 + (z // 2) * 2 + c) * 2 + z % 2


def column_pairs(shift, flip):
    return [
        (device_of(a, (z + shift) % 8, c ^ flip), device_of(a, z, c))
        for a in range(16)
        for z in range(8)
        for c in range(2)
    ]


def mirror_pairs(a_from, g_from):
    return [
        ((((a_from - a) % 16) * 8 + (g_from - g) % 8) * 2 + 1 - h, (a * 8 + g) * 2 + h)
        for a in range(16)
        for g in range(8)
        for h in range(2)
    ]


def gather_column(block):
    def receive(values, shift, flip=0):
        return lax.ppermute(values, AXES, column_pairs(shift, flip))

    held = {0: block}
    for shift in (1, 7, 2, 6):
        held[shift] = receive(block, shift)
    held[3] = receive(held[2], 1)
    held[5] = receive(held[6], 7)
    held[4] = receive(held[2], 2)
    blocks = []
    for shift in SHIFTS:
        blocks += [held[shift], receive(held[shift], 0, 1)]
    return blocks


def shape(dims, dtype):
    return jax.ShapeDtypeStruct(dims, dtype)


def body(current, kernel):
    g = lax.axis_index("gz")
    h = lax.axis_index("gy")
    info = jnp.stack([(g // 2) * 2 + h, g % 2, h, 0]).astype(jnp.int32)
    parity = jnp.arange(384) % 2
    sign = jnp.where((parity == 1) & (h == 1), -1.0, 1.0).astype(F32)
    flip, order, eye = mirror_tables()

    block = call(raw_kernel, shape((48, 1152), BF), [pltpu.VMEM((48, 1152), F32)], vmem=8)(current)
    blocks = gather_column(block)

    sent = call(
        weight_send_kernel,
        [shape((n, 48, 1152), BF) for n in PARTS]
        + [shape((48, 1152), BF), shape((32, 1152), BF), shape((16, 1152), BF)],
        [pltpu.VMEM((48, 1152), F32), pltpu.VMEM((40, 1152), F32)],
        in_specs=[pl.BlockSpec((6, 12, 4608), lambda n: (0, 0, 1))],
        grid=(1,),
        vmem=16,
    )(kernel)
    places = ((15, 7),) * len(PARTS) + ((16, 7), (15, 8), (16, 8))
    arrived = [lax.ppermute(s, AXES, mirror_pairs(*place)) for s, place in zip(sent, places)]
    own_weight = call(
        weight_own_kernel,
        shape((8, 192, 256), F32),
        [pltpu.VMEM((8, 256, 192), F32)],
        in_specs=[pl.BlockSpec((6, 12, 4864), lambda n: (0, 0, 0)), vmem_spec()],
        grid=(1,),
        vmem=24,
    )(kernel, jnp.asarray(eye))

    ta = jnp.asarray(first_forward()) * sign.astype(BF)[None, :, None]
    tb = lax.dynamic_index_in_dim(jnp.asarray(second_forward()), g, 0, keepdims=False)
    values = call(
        forward_kernel,
        shape((16, 6, 16, 256), BF),
        [
            pltpu.VMEM((6, 8, 48, 384), BF),
            pltpu.VMEM((6, 384, 640), BF),
            pltpu.VMEM((2, 1536, 128), F32),
        ],
        in_specs=[smem_spec()] + [vmem_spec()] * 19,
    )(info, *blocks, ta, tb, jnp.asarray(third_forward()))
    values = lax.all_to_all(values, "ta", split_axis=0, concat_axis=0, tiled=True)

    weight = call(
        weight_pair_kernel,
        shape((8, 192, 256), F32),
        [
            pltpu.VMEM((8, 256, 192), F32),
            pltpu.VMEM((48, 1152), F32),
            pltpu.VMEM((48, 1152), F32),
        ],
        vmem=24,
    )(own_weight, *arrived, jnp.asarray(flip), jnp.asarray(order))
    values = call(time_kernel, shape((16, 6, 16, 256), BF))(
        values, weight, jnp.asarray(time_forward()), jnp.asarray(time_inverse())
    )
    values = lax.all_to_all(values, "ta", split_axis=0, concat_axis=0, tiled=True)
    values = call(third_kernel, shape((8, 6, 16, 256), BF), [pltpu.VMEM((2, 1536, 128), F32)])(
        values, jnp.asarray(third_inverse())
    )
    values = lax.all_to_all(values, "gz", split_axis=0, concat_axis=0, tiled=True)
    own, send = call(
        last_kernel,
        [shape((6, 6, 1152), F32), shape((48, 1152), BF)],
        [
            pltpu.VMEM((2, 768, 128), F32),
            pltpu.VMEM((768, 128), F32),
            pltpu.VMEM((2, 48, 1152), F32),
        ],
        in_specs=[smem_spec()] + [vmem_spec()] * 4,
    )(info, values, jnp.asarray(second_inverse()), jnp.asarray(first_inverse()), sign[None, :])
    other = lax.ppermute(send, "gy", [(0, 1), (1, 0)])
    return call(sum_kernel, shape((6, 6, 1152), F32), vmem=8)(own, other)


def solution(mesh):
    specs = P("ta", "gz", "gy")
    return jax.shard_map(
        body, mesh=mesh, in_specs=(specs, specs), out_specs=specs, check_vma=False
    )
```

```python
import numpy as np

import jax
import jax.numpy as jnp
from jax import lax
from jax.experimental import pallas as pl
from jax.experimental.pallas import tpu as pltpu
from jax.sharding import PartitionSpec as P


BF = jnp.bfloat16
F32 = jnp.float32
AXES = ("ta", "gz", "gy")
PARTS = (5,)
SHIFTS = (0, 1, 7, 2, 6, 3, 5, 4)


def split_table(table, parts=2):
    table = np.asarray(table, np.float32)
    upper = table.astype(jnp.bfloat16)
    if parts == 1:
        return upper[None]
    lower = (table - upper.astype(np.float32)).astype(jnp.bfloat16)
    return np.stack([upper, lower])


def turn(numerator, period, sign):
    angle = 2.0 * np.pi * (np.asarray(numerator) % period) / period
    cosine, sine = np.cos(angle), sign * np.sin(angle)
    return np.stack([np.stack([cosine, -sine]), np.stack([sine, cosine])])


def first_forward():
    x = np.arange(48)
    i = np.arange(25)
    parts = turn(x[:, None] * i[None, :], 96, -1.0)[:, 0]
    table = np.zeros((8, 48, 5, 128))
    for y in range(8):
        block = parts.reshape(2, 48, 5, 5).transpose(1, 2, 0, 3).reshape(48, 5, 10)
        table[y, :, :, y * 10 : y * 10 + 10] = block
    return split_table(table.reshape(384, 640), 1)


def second_forward():
    y = np.arange(48)
    out = np.zeros((8, 6, 128, 2, 64))
    for g in range(8):
        q = 12 * g + np.arange(12)
        parts = turn(y[:, None] * q[None, :], 96, -1.0)
        for i in range(5):
            for inp in range(2):
                for r in range(8):
                    out[g, :, r * 10 + inp * 5 + i, :, i * 12 : i * 12 + 12] = parts[
                        :, inp, r::8
                    ].transpose(1, 0, 2)
    table = split_table(out.reshape(8, 768, 128))
    return np.concatenate([table[0], table[1]], axis=2)


def third_forward():
    w = np.arange(96)
    z = np.arange(48)
    parts = turn(w[:, None] * z[None, :], 96, -1.0)
    table = np.zeros((96, 2, 2, 8, 8))
    table[..., :6] = parts.transpose(2, 0, 1, 3).reshape(96, 2, 2, 8, 6)
    return split_table(table.reshape(192, 128))


def time_forward():
    k = np.arange(192)
    t = np.arange(96)
    parts = turn(k[:, None] * t[None, :], 192, -1.0)
    parts = parts.transpose(0, 2, 3, 1).reshape(2, 192, 16, 6, 2).transpose(0, 1, 2, 4, 3)
    table = np.zeros((4, 2, 192, 16, 2, 8))
    table[0, ..., :6] = parts
    for s in range(3):
        table[1 + s, ..., 6:8] = parts[..., 2 * s : 2 * s + 2]
    return split_table(table.reshape(4, 384, 256), 1)


def time_inverse():
    k = np.arange(192)
    t = np.arange(96)
    parts = turn(t[:, None] * k[None, :], 192, 1.0) / 192.0
    parts = parts.reshape(2, 2, 16, 6, 192).transpose(2, 0, 3, 1, 4)
    table = np.zeros((4, 16, 2, 8, 2, 192))
    table[0, :, :, :6] = parts
    for s in range(3):
        table[1 + s, :, :, 6:8] = parts[:, :, 2 * s : 2 * s + 2]
    return split_table(table.reshape(4, 256, 384), 1)


def third_inverse():
    w = np.arange(96)
    z = np.arange(48)
    parts = turn(z[:, None] * w[None, :], 96, 1.0) / 96.0
    parts = parts.reshape(2, 2, 8, 6, 96).transpose(2, 0, 3, 4, 1)
    table = np.zeros((4, 8, 2, 8, 96, 2))
    table[0, :, :, :6] = parts
    for s in range(3):
        table[1 + s, :, :, 6:8] = parts[:, :, 2 * s : 2 * s + 2]
    return split_table(table.reshape(4, 128, 192))


def second_inverse():
    q = np.arange(96)
    y = np.arange(48)
    parts = turn(q[:, None] * y[None, :], 96, 1.0) / 96.0
    parts = parts.reshape(2, 2, 8, 12, 6, 8)
    table = np.zeros((8, 2, 64, 6, 128))
    for i in range(5):
        for r in range(8):
            for out in range(2):
                table[:, :, i * 12 : i * 12 + 12, :, r * 10 + out * 5 + i] = parts[
                    out, :, :, :, :, r
                ].transpose(1, 0, 2, 3)
    return split_table(table.reshape(1024, 768), 1)


def first_inverse():
    i = np.arange(25)
    x = np.arange(48)
    parts = turn(i[:, None] * x[None, :], 96, 1.0)[0] / 96.0
    table = np.zeros((5, 128, 8, 48))
    for r in range(8):
        for inp in range(2):
            table[:, r * 10 + inp * 5 : r * 10 + inp * 5 + 5, r] = parts[inp].reshape(5, 5, 48)
    return split_table(table.reshape(640, 384))


def mirror_tables():
    flip = np.zeros((192, 192))
    flip[np.arange(192), (-np.arange(192)) % 192] = 1.0
    order = np.zeros((256, 256))
    for group in range(4):
        for i in range(5):
            for q in range(12):
                row = group * 64 + i * 12
                order[row + q, row + (12 - q) % 12] = 1.0
    return flip.astype(jnp.bfloat16), order.astype(jnp.bfloat16), np.eye(192).astype(jnp.bfloat16)


def dot(left, right):
    return lax.dot_general(left, right, (((1,), (0,)), ((), ())), preferred_element_type=F32)


def dot_table(table_ref, rows, *place):
    total = dot(table_ref[(0, *place)], rows)
    for n in range(1, table_ref.shape[0]):
        total = total + dot(table_ref[(n, *place)], rows)
    return total


def dot_columns(rows, table_ref):
    total = dot(rows, table_ref[0])
    for n in range(1, table_ref.shape[0]):
        total = total + dot(rows, table_ref[n])
    return total


def start_copies(sources, targets, arrival):
    copies = [
        pltpu.make_async_copy(source, target, arrival.at[n])
        for n, (source, target) in enumerate(zip(sources, targets))
    ]
    for copy in copies:
        copy.start()
    return copies


def dot_rows(left, right):
    return lax.dot_general(left, right, (((1,), (1,)), ((), ())), preferred_element_type=F32)


def low_half(shape):
    return lax.broadcasted_iota(jnp.int32, shape, 1) % 128 < 64


def swap_half(values):
    return pltpu.roll(values, 64, 1)


def call(kernel, out_shape, scratch=(), in_specs=None, grid=(), vmem=14, flops=10**8, moved=4 * 10**6):
    placed = {} if in_specs is None else {"in_specs": in_specs}
    return pl.pallas_call(
        kernel,
        out_shape=out_shape,
        **placed,
        grid=grid,
        scratch_shapes=list(scratch),
        compiler_params=pltpu.CompilerParams(vmem_limit_bytes=vmem * 2**20),
        cost_estimate=pl.CostEstimate(flops=flops, bytes_accessed=moved, transcendentals=0),
    )


def vmem_spec():
    return pl.BlockSpec(memory_space=pltpu.VMEM)


def smem_spec():
    return pl.BlockSpec(memory_space=pltpu.SMEM)


def raw_kernel(current_ref, out_ref, work):
    work[...] = jnp.zeros_like(work)
    for t in range(6):
        work[8 * t : 8 * t + 6, :] = current_ref[t]
    out_ref[...] = work[...].astype(BF)


def part_of(plane):
    for part, count in enumerate(PARTS):
        if plane < count:
            return part, plane
        plane -= count


def weight_send_kernel(source_ref, *refs):
    refs = refs[16:]
    plane_ref, line_ref, corner_ref, work, rows, kernel_ref, arrival = refs[len(PARTS) :]
    copy = pltpu.make_async_copy(source_ref.at[:, :, pl.ds(4608, 4608)], kernel_ref, arrival)
    copy.start()
    copy.wait()
    rows[...] = jnp.zeros_like(rows)
    for w in range(6):
        for c in range(4):
            piece = kernel_ref[w, :, 1152 * c : 1152 * (c + 1)]
            work[12 * c : 12 * c + 12, :] = piece
            rows[4 * w + c : 4 * w + c + 1, :] = piece[0:1]
        if w == 0:
            plane_ref[...] = work[...].astype(BF)
        else:
            part, place = part_of(w - 1)
            refs[part][place] = work[...].astype(BF)
    line_ref[...] = rows[4:28, :].astype(BF)
    corner_ref[...] = rows[0:8, :].astype(BF)


def own_weights(kernel_ref, eye_ref, weight, work):
    eye = eye_ref[...]
    work[...] = jnp.zeros_like(work)
    for w in range(6):
        for i in range(25):
            piece = kernel_ref[w, :, 192 * i : 192 * (i + 1)]
            row = 64 * (i // 5) + 12 * (i % 5)
            if i < 20:
                work[w, row : row + 12, :] = piece
            else:
                row = 64 * (w // 2) + 12 * (i % 5)
                work[6 + w % 2, row : row + 12, :] = piece
    for v in range(8):
        values = work[v]
        upper = values.astype(BF)
        lower = (values - upper.astype(F32)).astype(BF)
        weight[v] = dot_rows(eye, upper) + dot_rows(eye, lower)


def pair_weights(refs, flip_ref, order_ref, weight, work, held, rows):
    plane_ref, line_ref, corner_ref = refs[len(PARTS) :]
    flip, order = flip_ref[...], order_ref[...]
    work[...] = jnp.zeros_like(work)
    rows[0:8, :] = corner_ref[...].astype(F32)
    rows[8:32, :] = line_ref[...].astype(F32)
    for w in range(6):
        if w == 0:
            held[...] = plane_ref[...].astype(F32)
            first = 0
        else:
            part, place = part_of(5 - w)
            held[...] = refs[part][place].astype(F32)
            first = 8 + 4 * (5 - w)
        for i in range(1, 24):
            c, p = (24 - i) // 6, (24 - i) % 6
            piece = held[12 * c : 12 * c + 12, 192 * p : 192 * (p + 1)]
            line = rows[first + c : first + c + 1, 192 * p : 192 * (p + 1)]
            if i < 20:
                v, row = w, 64 * (i // 5) + 12 * (i % 5)
            else:
                v, row = 6 + w % 2, 64 * (w // 2) + 12 * (i % 5)
            work[v, row : row + 12, :] = piece
            work[v, row : row + 1, :] = line
    for v in range(8):
        turned = dot(order, work[v].astype(BF)).astype(BF)
        weight[v] = weight[v] + dot_rows(flip, turned)


def put_rows(work, row, count, values):
    work[0, pl.ds(row, count, stride=8), :] = values[:, :128]
    work[1, pl.ds(row, count, stride=8), :] = values[:, 128:]


def get_rows(work, row, count):
    halves = [work[n, pl.ds(row, count, stride=8), :] for n in range(2)]
    return jnp.concatenate(halves, axis=1)


def forward_kernel(info_ref, sign_ref, *refs):
    sources = list(refs[:19])
    sources[17] = sources[17].at[info_ref[3]]
    out_ref, raw, half, work, blocks, ta_ref, tb_ref, t3_ref, arrival = refs[19:]
    targets = [blocks.at[n] for n in range(16)] + [ta_ref, tb_ref, t3_ref]
    copies = start_copies(sources, targets, arrival)
    for copy in copies[:17]:
        copy.wait()
    place, core = info_ref[0], info_ref[1]
    for n in range(16):
        spot = lax.rem(place + SHIFTS[n // 2], 8)
        side = lax.rem(spot, 2)
        plane = (spot // 2) * 2 + (core if n % 2 == 0 else 1 - core)
        for y in range(3):
            raw[side * 3 + y, plane] = blocks[n, :, 384 * y : 384 * (y + 1)]
    for y in range(6):
        rows = raw[y].reshape(384, 384)
        rows = (rows.astype(F32) * sign_ref[...]).astype(BF)
        half[y] = dot_columns(rows, ta_ref).astype(BF)
    for copy in copies[17:]:
        copy.wait()
    seconds = []
    for ig in range(5):
        merged = jnp.concatenate([half[y, :, 128 * ig : 128 * (ig + 1)] for y in range(6)], axis=1)
        both = dot(merged, tb_ref[...])
        seconds.append(both[:, :128] + both[:, 128:])
    low = low_half((384, 128))
    real_main, imag_main = [], []
    for pair in range(2):
        left, right = seconds[2 * pair], seconds[2 * pair + 1]
        real_main.append(jnp.where(low, left, swap_half(right)))
        imag_main.append(jnp.where(low, swap_half(left), right))
    real_main = jnp.concatenate(real_main, axis=1).reshape(8, 6, 8, 256)
    imag_main = jnp.concatenate(imag_main, axis=1).reshape(8, 6, 8, 256)
    last = seconds[4].reshape(8, 6, 8, 128)
    turned = swap_half(seconds[4]).reshape(8, 6, 8, 128)
    low = low_half((64, 128))

    def finish(row, real_part, imag_part):
        merged = jnp.concatenate([real_part, imag_part], axis=0).astype(BF)
        put_rows(work, row, 192, dot_table(t3_ref, merged))

    for t in range(6):
        finish(t, real_main[:, t].reshape(64, 256), imag_main[:, t].reshape(64, 256))
    for e in range(2):
        plain = [last[:, e + 2 * s].reshape(64, 128) for s in range(3)]
        moved = [turned[:, e + 2 * s].reshape(64, 128) for s in range(3)]
        real_part = [jnp.where(low, plain[0], moved[1]), jnp.where(low, plain[2], 0.0)]
        imag_part = [jnp.where(low, moved[0], plain[1]), jnp.where(low, moved[2], 0.0)]
        finish(6 + e, jnp.concatenate(real_part, axis=1), jnp.concatenate(imag_part, axis=1))
    merged = jnp.concatenate([work[0], work[1]], axis=1)
    out_ref[...] = merged.reshape(16, 6, 16, 256).astype(BF)


def gather_groups(pieces):
    pieces = pieces + [jnp.zeros_like(pieces[0])]
    return jnp.concatenate(pieces, axis=1)


def time_kernel(*refs):
    count = len(PARTS) + 10
    sources, out_ref, targets = refs[:count], refs[count], refs[count + 1 : 2 * count + 1]
    work, held, rows, weight, arrival = refs[2 * count + 1 :]
    sources = list(sources)
    sources[0] = sources[0].at[:, :, pl.ds(0, 4864)]
    copies = start_copies(sources, targets, arrival)
    eye_ref, flip_ref, order_ref, forward_ref, inverse_ref, in_ref = targets[count - 6 :]
    for copy in copies[: count - 3]:
        copy.wait()
    own_weights(targets[0], eye_ref, weight, work)
    pair_weights(targets[1 : count - 6], flip_ref, order_ref, weight, work, held, rows)
    for copy in copies[count - 3 :]:
        copy.wait()

    def weighted(values, v):
        part = weight[v]
        return (values * jnp.concatenate([part, part], axis=0)).astype(BF)

    def forward(rows, n):
        return dot_table(forward_ref, rows, n)

    def inverse(rows, n):
        return dot_table(inverse_ref, rows, n)

    loaded = [in_ref[:, w].reshape(256, 256) for w in range(6)]
    for e in range(2):
        total = None
        for s in range(3):
            rows = gather_groups([loaded[2 * r + e][:, 64 * s : 64 * (s + 1)] for r in range(3)])
            term = forward(rows, 1 + s)
            total = term if total is None else total + term
        spectrum = weighted(total, 6 + e)
        tails = [inverse(spectrum, 1 + s) for s in range(3)]
        for r in range(3):
            w = 2 * r + e
            values = inverse(weighted(forward(loaded[w], 0), w), 0)
            values = values + gather_groups([tail[:, 64 * r : 64 * (r + 1)] for tail in tails])
            out_ref[:, w] = values.astype(BF).reshape(16, 16, 256)


def third_kernel(in_ref, table_ref, out_ref, work):
    values = in_ref[...].astype(F32).reshape(1536, 256)
    work[0] = values[:, :128]
    work[1] = values[:, 128:]

    def inverse(rows, n):
        return dot(table_ref[0, n], rows) + dot(table_ref[1, n], rows)

    def load(row):
        return get_rows(work, row, 192).astype(BF)

    for e in range(2):
        rows = load(6 + e)
        tails = [inverse(rows, 1 + s) for s in range(3)]
        for r in range(3):
            t = 2 * r + e
            values = inverse(load(t), 0)
            values = values + gather_groups([tail[:, 64 * r : 64 * (r + 1)] for tail in tails])
            out_ref[:, t] = values.astype(BF).reshape(8, 16, 256)


def last_kernel(
    info_ref, in_ref, tb_source, ta_source, sign_ref, own_ref, send_ref, work, spare, both,
    tb_ref, ta_ref, arrival
):
    copies = start_copies((tb_source, ta_source), (tb_ref, ta_ref), arrival)
    side = info_ref[2]
    values = in_ref[...].astype(F32).reshape(768, 256)
    work[0] = values[:, :128]
    work[1] = values[:, 128:]
    spare[...] = jnp.zeros_like(spare)
    for e in range(2):
        rows = get_rows(work, 6 + e, 96)
        spare[pl.ds(e, 96, stride=8), :] = rows[:, :128]
        spare[pl.ds(2 + e, 96, stride=8), :] = swap_half(rows[:, :128])
        spare[pl.ds(4 + e, 96, stride=8), :] = rows[:, 128:]
    low = low_half((48, 128))
    groups = [[] for _ in range(5)]
    shaped = values.reshape(8, 6, 2, 8, 256)
    shaped_spare = spare[...].reshape(8, 6, 2, 8, 128)
    for g in range(8):
        real_part = shaped[g, :, 0].reshape(48, 256)
        imag_part = shaped[g, :, 1].reshape(48, 256)
        for pair in range(2):
            real_tile = real_part[:, 128 * pair : 128 * (pair + 1)]
            imag_tile = imag_part[:, 128 * pair : 128 * (pair + 1)]
            groups[2 * pair].append(jnp.where(low, real_tile, swap_half(imag_tile)))
            groups[2 * pair + 1].append(jnp.where(low, swap_half(real_tile), imag_tile))
        real_tile = shaped_spare[g, :, 0].reshape(48, 128)
        imag_tile = shaped_spare[g, :, 1].reshape(48, 128)
        groups[4].append(jnp.where(low, real_tile, swap_half(imag_tile)))
    rows = jnp.concatenate([jnp.concatenate(group, axis=1) for group in groups], axis=0).astype(BF)
    for copy in copies:
        copy.wait()
    half = dot_columns(rows, tb_ref).astype(BF)
    rows = jnp.concatenate(
        [
            jnp.concatenate(
                [half[48 * ig : 48 * (ig + 1), 128 * y : 128 * (y + 1)] for ig in range(5)], axis=1
            )
            for y in range(6)
        ],
        axis=0,
    )
    result = dot_columns(rows, ta_ref) * sign_ref[...]
    for y in range(6):
        both[y // 3, :, 384 * (y % 3) : 384 * (y % 3 + 1)] = result[48 * y : 48 * (y + 1)]
    own = both[side]
    for t in range(6):
        own_ref[t] = own[8 * t : 8 * t + 6]
    send_ref[...] = both[1 - side].astype(BF)


def sum_kernel(own_ref, other_ref, out_ref):
    other = other_ref[...].astype(F32)
    for t in range(6):
        out_ref[t] = own_ref[t] + other[8 * t : 8 * t + 6]


def device_of(a, z, c):
    return (a * 8 + (z // 2) * 2 + c) * 2 + z % 2


def column_pairs(shift, flip):
    return [
        (device_of(a, (z + shift) % 8, c ^ flip), device_of(a, z, c))
        for a in range(16)
        for z in range(8)
        for c in range(2)
    ]


def mirror_pairs(a_from, g_from):
    return [
        ((((a_from - a) % 16) * 8 + (g_from - g) % 8) * 2 + 1 - h, (a * 8 + g) * 2 + h)
        for a in range(16)
        for g in range(8)
        for h in range(2)
    ]


def gather_column(block):
    def receive(values, shift, flip=0):
        return lax.ppermute(values, AXES, column_pairs(shift, flip))

    held = {0: block}
    for shift in (1, 7, 2, 6):
        held[shift] = receive(block, shift)
    held[3] = receive(held[2], 1)
    held[5] = receive(held[6], 7)
    held[4] = receive(held[2], 2)
    blocks = []
    for shift in SHIFTS:
        blocks += [held[shift], receive(held[shift], 0, 1)]
    return blocks


def shape(dims, dtype):
    return jax.ShapeDtypeStruct(dims, dtype)


def body(current, kernel):
    g = lax.axis_index("gz")
    h = lax.axis_index("gy")
    info = jnp.stack([(g // 2) * 2 + h, g % 2, h, g]).astype(jnp.int32)
    parity = jnp.arange(384) % 2
    sign = jnp.where((parity == 1) & (h == 1), -1.0, 1.0).astype(F32)
    flip, order, eye = mirror_tables()

    anywhere = pl.BlockSpec(memory_space=pl.ANY)
    block = call(raw_kernel, shape((48, 1152), BF), [pltpu.VMEM((48, 1152), F32)], vmem=8)(current)
    blocks = gather_column(block)

    sent = call(
        weight_send_kernel,
        [shape((n, 48, 1152), BF) for n in PARTS]
        + [shape((48, 1152), BF), shape((24, 1152), BF), shape((8, 1152), BF)],
        [pltpu.VMEM((48, 1152), F32), pltpu.VMEM((32, 1152), F32)]
        + [pltpu.VMEM((6, 12, 4608), F32), pltpu.SemaphoreType.DMA],
        in_specs=[anywhere] * 17,
        vmem=59,
    )(kernel, *blocks)
    places = ((15, 7),) * len(PARTS) + ((16, 7), (15, 8), (16, 8))
    arrived = [lax.ppermute(s, AXES, mirror_pairs(*place)) for s, place in zip(sent, places)]
    def spread(*operands):
        values = call(
            forward_kernel,
            shape((16, 6, 16, 256), BF),
            [
                pltpu.VMEM((6, 8, 48, 384), BF),
                pltpu.VMEM((6, 384, 640), BF),
                pltpu.VMEM((2, 1536, 128), F32),
                pltpu.VMEM((16, 48, 1152), BF),
                pltpu.VMEM((1, 384, 640), BF),
                pltpu.VMEM((768, 256), BF),
                pltpu.VMEM((2, 192, 128), BF),
                pltpu.SemaphoreType.DMA((19,)),
            ],
            in_specs=[smem_spec(), vmem_spec()] + [anywhere] * 19,
            vmem=59,
        )(*operands)
        return lax.all_to_all(values, "ta", split_axis=0, concat_axis=0, tiled=True)

    values = lax.cond(
        g < lax.axis_size("gz"),
        spread,
        lambda *operands: jnp.zeros((16, 6, 16, 256), BF),
        info, sign[None, :], *blocks, jnp.asarray(first_forward()), jnp.asarray(second_forward()),
        jnp.asarray(third_forward()),
    )
    operands = (
        kernel, *arrived, jnp.asarray(eye), jnp.asarray(flip), jnp.asarray(order),
        jnp.asarray(time_forward()), jnp.asarray(time_inverse()), values
    )
    values = call(
        time_kernel,
        shape((16, 6, 16, 256), BF),
        [pltpu.VMEM((6, 12, 4864), F32)]
        + [pltpu.VMEM(operand.shape, operand.dtype) for operand in operands[1:]]
        + [
            pltpu.VMEM((8, 256, 192), F32),
            pltpu.VMEM((48, 1152), F32),
            pltpu.VMEM((32, 1152), F32),
            pltpu.VMEM((8, 192, 256), F32),
            pltpu.SemaphoreType.DMA((len(operands),)),
        ],
        in_specs=[anywhere] * len(operands),
        vmem=59,
    )(*operands)
    values = lax.all_to_all(values, "ta", split_axis=0, concat_axis=0, tiled=True)
    values = call(third_kernel, shape((8, 6, 16, 256), BF), [pltpu.VMEM((2, 1536, 128), F32)])(
        values, jnp.asarray(third_inverse())
    )
    values = lax.all_to_all(values, "gz", split_axis=0, concat_axis=0, tiled=True)
    own, send = call(
        last_kernel,
        [shape((6, 6, 1152), F32), shape((48, 1152), BF)],
        [
            pltpu.VMEM((2, 768, 128), F32),
            pltpu.VMEM((768, 128), F32),
            pltpu.VMEM((2, 48, 1152), F32),
            pltpu.VMEM((1, 1024, 768), BF),
            pltpu.VMEM((2, 640, 384), BF),
            pltpu.SemaphoreType.DMA((2,)),
        ],
        in_specs=[smem_spec(), vmem_spec(), anywhere, anywhere, vmem_spec()],
    )(info, values, jnp.asarray(second_inverse()), jnp.asarray(first_inverse()), sign[None, :])
    other = lax.ppermute(send, "gy", [(0, 1), (1, 0)])
    return call(sum_kernel, shape((6, 6, 1152), F32), vmem=8)(own, other)


def solution(mesh):
    specs = P("ta", "gz", "gy")
    return jax.shard_map(
        body, mesh=mesh, in_specs=(specs, specs), out_specs=specs, check_vma=False
    )
```

```python
import numpy as np

import jax
import jax.numpy as jnp
from jax import lax
from jax.experimental import pallas as pl
from jax.experimental.pallas import tpu as pltpu
from jax.sharding import PartitionSpec as P


BF = jnp.bfloat16
F32 = jnp.float32
AXES = ("ta", "gz", "gy")
PARTS = (5,)
SHIFTS = (0, 1, 7, 2, 6, 3, 5, 4)


def split_table(table, parts=2):
    table = np.asarray(table, np.float32)
    upper = table.astype(jnp.bfloat16)
    if parts == 1:
        return upper[None]
    lower = (table - upper.astype(np.float32)).astype(jnp.bfloat16)
    return np.stack([upper, lower])


def turn(numerator, period, sign):
    angle = 2.0 * np.pi * (np.asarray(numerator) % period) / period
    cosine, sine = np.cos(angle), sign * np.sin(angle)
    return np.stack([np.stack([cosine, -sine]), np.stack([sine, cosine])])


def first_forward():
    x = np.arange(48)
    i = np.arange(25)
    parts = turn(x[:, None] * i[None, :], 96, -1.0)[:, 0]
    table = np.zeros((8, 48, 5, 128))
    for y in range(8):
        block = parts.reshape(2, 48, 5, 5).transpose(1, 2, 0, 3).reshape(48, 5, 10)
        table[y, :, :, y * 10 : y * 10 + 10] = block
    return split_table(table.reshape(384, 640), 1)


def second_forward():
    y = np.arange(48)
    out = np.zeros((8, 6, 128, 2, 64))
    for g in range(8):
        q = 12 * g + np.arange(12)
        parts = turn(y[:, None] * q[None, :], 96, -1.0)
        for i in range(5):
            for inp in range(2):
                for r in range(8):
                    out[g, :, r * 10 + inp * 5 + i, :, i * 12 : i * 12 + 12] = parts[
                        :, inp, r::8
                    ].transpose(1, 0, 2)
    table = split_table(out.reshape(8, 768, 128))
    return np.concatenate([table[0], table[1]], axis=2)


def third_forward():
    w = np.arange(96)
    z = np.arange(48)
    parts = turn(w[:, None] * z[None, :], 96, -1.0)
    table = np.zeros((96, 2, 2, 8, 8))
    table[..., :6] = parts.transpose(2, 0, 1, 3).reshape(96, 2, 2, 8, 6)
    return split_table(table.reshape(192, 128))


def time_forward():
    k = np.arange(192)
    t = np.arange(96)
    parts = turn(k[:, None] * t[None, :], 192, -1.0)
    parts = parts.transpose(0, 2, 3, 1).reshape(2, 192, 16, 6, 2).transpose(0, 1, 2, 4, 3)
    table = np.zeros((4, 2, 192, 16, 2, 8))
    table[0, ..., :6] = parts
    for s in range(3):
        table[1 + s, ..., 6:8] = parts[..., 2 * s : 2 * s + 2]
    return split_table(table.reshape(4, 384, 256), 1)


def time_inverse():
    k = np.arange(192)
    t = np.arange(96)
    parts = turn(t[:, None] * k[None, :], 192, 1.0) / 192.0
    parts = parts.reshape(2, 2, 16, 6, 192).transpose(2, 0, 3, 1, 4)
    table = np.zeros((4, 16, 2, 8, 2, 192))
    table[0, :, :, :6] = parts
    for s in range(3):
        table[1 + s, :, :, 6:8] = parts[:, :, 2 * s : 2 * s + 2]
    return split_table(table.reshape(4, 256, 384), 1)


def third_inverse():
    w = np.arange(96)
    z = np.arange(48)
    parts = turn(z[:, None] * w[None, :], 96, 1.0) / 96.0
    parts = parts.reshape(2, 2, 8, 6, 96).transpose(2, 0, 3, 4, 1)
    table = np.zeros((4, 8, 2, 8, 96, 2))
    table[0, :, :, :6] = parts
    for s in range(3):
        table[1 + s, :, :, 6:8] = parts[:, :, 2 * s : 2 * s + 2]
    return split_table(table.reshape(4, 128, 192))


def second_inverse():
    q = np.arange(96)
    y = np.arange(48)
    parts = turn(q[:, None] * y[None, :], 96, 1.0) / 96.0
    parts = parts.reshape(2, 2, 8, 12, 6, 8)
    table = np.zeros((8, 2, 64, 6, 128))
    for i in range(5):
        for r in range(8):
            for out in range(2):
                table[:, :, i * 12 : i * 12 + 12, :, r * 10 + out * 5 + i] = parts[
                    out, :, :, :, :, r
                ].transpose(1, 0, 2, 3)
    return split_table(table.reshape(1024, 768), 1)


def first_inverse():
    i = np.arange(25)
    x = np.arange(48)
    parts = turn(i[:, None] * x[None, :], 96, 1.0)[0] / 96.0
    table = np.zeros((5, 128, 8, 48))
    for r in range(8):
        for inp in range(2):
            table[:, r * 10 + inp * 5 : r * 10 + inp * 5 + 5, r] = parts[inp].reshape(5, 5, 48)
    return split_table(table.reshape(640, 384))


def mirror_tables():
    flip = np.zeros((192, 192))
    flip[np.arange(192), (-np.arange(192)) % 192] = 1.0
    order = np.zeros((256, 256))
    for group in range(4):
        for i in range(5):
            for q in range(12):
                row = group * 64 + i * 12
                order[row + q, row + (12 - q) % 12] = 1.0
    return flip.astype(jnp.bfloat16), order.astype(jnp.bfloat16), np.eye(192).astype(jnp.bfloat16)


def dot(left, right):
    return lax.dot_general(left, right, (((1,), (0,)), ((), ())), preferred_element_type=F32)


def dot_table(table_ref, rows, *place):
    total = dot(table_ref[(0, *place)], rows)
    for n in range(1, table_ref.shape[0]):
        total = total + dot(table_ref[(n, *place)], rows)
    return total


def dot_columns(rows, table_ref):
    total = dot(rows, table_ref[0])
    for n in range(1, table_ref.shape[0]):
        total = total + dot(rows, table_ref[n])
    return total


def start_copies(sources, targets, arrival):
    copies = [
        pltpu.make_async_copy(source, target, arrival.at[n])
        for n, (source, target) in enumerate(zip(sources, targets))
    ]
    for copy in copies:
        copy.start()
    return copies


def dot_rows(left, right):
    return lax.dot_general(left, right, (((1,), (1,)), ((), ())), preferred_element_type=F32)


def low_half(shape):
    return lax.broadcasted_iota(jnp.int32, shape, 1) % 128 < 64


def swap_half(values):
    return pltpu.roll(values, 64, 1)


def call(kernel, out_shape, scratch=(), in_specs=None, grid=(), vmem=14, flops=10**8, moved=4 * 10**6):
    placed = {} if in_specs is None else {"in_specs": in_specs}
    return pl.pallas_call(
        kernel,
        out_shape=out_shape,
        **placed,
        grid=grid,
        scratch_shapes=list(scratch),
        compiler_params=pltpu.CompilerParams(vmem_limit_bytes=vmem * 2**20),
        cost_estimate=pl.CostEstimate(flops=flops, bytes_accessed=moved, transcendentals=0),
    )


def vmem_spec():
    return pl.BlockSpec(memory_space=pltpu.VMEM)


def smem_spec():
    return pl.BlockSpec(memory_space=pltpu.SMEM)


def raw_kernel(current_ref, out_ref, work):
    work[...] = jnp.zeros_like(work)
    for t in range(6):
        work[8 * t : 8 * t + 6, :] = current_ref[t]
    out_ref[...] = work[...].astype(BF)


def part_of(plane):
    for part, count in enumerate(PARTS):
        if plane < count:
            return part, plane
        plane -= count


def weight_line_kernel(source_ref, line_ref, corner_ref, rows, kernel_ref, arrival):
    copy = pltpu.make_async_copy(
        source_ref.at[:, 0:8, pl.ds(4608, 4608)], kernel_ref, arrival
    )
    copy.start()
    copy.wait()
    rows[...] = jnp.zeros_like(rows)
    for w in range(6):
        for c in range(4):
            piece = kernel_ref[w, 0:1, 1152 * c : 1152 * (c + 1)]
            rows[4 * w + c : 4 * w + c + 1, :] = piece
    line_ref[...] = rows[4:28, :].astype(BF)
    corner_ref[...] = rows[0:8, :].astype(BF)


def weight_send_kernel(source_ref, *refs):
    refs = refs[18:]
    plane_ref, work, kernel_ref, arrival = refs[len(PARTS) :]
    copy = pltpu.make_async_copy(source_ref.at[:, :, pl.ds(4608, 4608)], kernel_ref, arrival)
    copy.start()
    copy.wait()
    for w in range(6):
        for c in range(4):
            piece = kernel_ref[w, :, 1152 * c : 1152 * (c + 1)]
            work[12 * c : 12 * c + 12, :] = piece
        if w == 0:
            plane_ref[...] = work[...].astype(BF)
        else:
            part, place = part_of(w - 1)
            refs[part][place] = work[...].astype(BF)


def own_weights(kernel_ref, eye_ref, weight, work):
    eye = eye_ref[...]
    work[...] = jnp.zeros_like(work)
    for w in range(6):
        for i in range(25):
            piece = kernel_ref[w, :, 192 * i : 192 * (i + 1)]
            row = 64 * (i // 5) + 12 * (i % 5)
            if i < 20:
                work[w, row : row + 12, :] = piece
            else:
                row = 64 * (w // 2) + 12 * (i % 5)
                work[6 + w % 2, row : row + 12, :] = piece
    for v in range(8):
        values = work[v]
        upper = values.astype(BF)
        lower = (values - upper.astype(F32)).astype(BF)
        weight[v] = dot_rows(eye, upper) + dot_rows(eye, lower)


def pair_weights(refs, flip_ref, order_ref, weight, work, held, rows):
    plane_ref, line_ref, corner_ref = refs[len(PARTS) :]
    flip, order = flip_ref[...], order_ref[...]
    work[...] = jnp.zeros_like(work)
    rows[0:8, :] = corner_ref[...].astype(F32)
    rows[8:32, :] = line_ref[...].astype(F32)
    for w in range(6):
        if w == 0:
            held[...] = plane_ref[...].astype(F32)
            first = 0
        else:
            part, place = part_of(5 - w)
            held[...] = refs[part][place].astype(F32)
            first = 8 + 4 * (5 - w)
        for i in range(1, 24):
            c, p = (24 - i) // 6, (24 - i) % 6
            piece = held[12 * c : 12 * c + 12, 192 * p : 192 * (p + 1)]
            line = rows[first + c : first + c + 1, 192 * p : 192 * (p + 1)]
            if i < 20:
                v, row = w, 64 * (i // 5) + 12 * (i % 5)
            else:
                v, row = 6 + w % 2, 64 * (w // 2) + 12 * (i % 5)
            work[v, row : row + 12, :] = piece
            work[v, row : row + 1, :] = line
    for v in range(8):
        turned = dot(order, work[v].astype(BF)).astype(BF)
        weight[v] = weight[v] + dot_rows(flip, turned)


def put_rows(work, row, count, values):
    work[0, pl.ds(row, count, stride=8), :] = values[:, :128]
    work[1, pl.ds(row, count, stride=8), :] = values[:, 128:]


def get_rows(work, row, count):
    halves = [work[n, pl.ds(row, count, stride=8), :] for n in range(2)]
    return jnp.concatenate(halves, axis=1)


def forward_kernel(info_ref, sign_ref, *refs):
    sources = list(refs[:19])
    sources[17] = sources[17].at[info_ref[3]]
    out_ref, raw, half, work, blocks, ta_ref, tb_ref, t3_ref, arrival = refs[19:]
    targets = [blocks.at[n] for n in range(16)] + [ta_ref, tb_ref, t3_ref]
    copies = start_copies(sources, targets, arrival)
    for copy in copies[:17]:
        copy.wait()
    place, core = info_ref[0], info_ref[1]
    for n in range(16):
        spot = lax.rem(place + SHIFTS[n // 2], 8)
        side = lax.rem(spot, 2)
        plane = (spot // 2) * 2 + (core if n % 2 == 0 else 1 - core)
        for y in range(3):
            raw[side * 3 + y, plane] = blocks[n, :, 384 * y : 384 * (y + 1)]
    for y in range(6):
        rows = raw[y].reshape(384, 384)
        rows = (rows.astype(F32) * sign_ref[...]).astype(BF)
        half[y] = dot_columns(rows, ta_ref).astype(BF)
    for copy in copies[17:]:
        copy.wait()
    seconds = []
    for ig in range(5):
        merged = jnp.concatenate([half[y, :, 128 * ig : 128 * (ig + 1)] for y in range(6)], axis=1)
        both = dot(merged, tb_ref[...])
        seconds.append(both[:, :128] + both[:, 128:])
    low = low_half((384, 128))
    real_main, imag_main = [], []
    for pair in range(2):
        left, right = seconds[2 * pair], seconds[2 * pair + 1]
        real_main.append(jnp.where(low, left, swap_half(right)))
        imag_main.append(jnp.where(low, swap_half(left), right))
    real_main = jnp.concatenate(real_main, axis=1).reshape(8, 6, 8, 256)
    imag_main = jnp.concatenate(imag_main, axis=1).reshape(8, 6, 8, 256)
    last = seconds[4].reshape(8, 6, 8, 128)
    turned = swap_half(seconds[4]).reshape(8, 6, 8, 128)
    low = low_half((64, 128))

    def finish(row, real_part, imag_part):
        merged = jnp.concatenate([real_part, imag_part], axis=0).astype(BF)
        put_rows(work, row, 192, dot_table(t3_ref, merged))

    for t in range(6):
        finish(t, real_main[:, t].reshape(64, 256), imag_main[:, t].reshape(64, 256))
    for e in range(2):
        plain = [last[:, e + 2 * s].reshape(64, 128) for s in range(3)]
        moved = [turned[:, e + 2 * s].reshape(64, 128) for s in range(3)]
        real_part = [jnp.where(low, plain[0], moved[1]), jnp.where(low, plain[2], 0.0)]
        imag_part = [jnp.where(low, moved[0], plain[1]), jnp.where(low, moved[2], 0.0)]
        finish(6 + e, jnp.concatenate(real_part, axis=1), jnp.concatenate(imag_part, axis=1))
    merged = jnp.concatenate([work[0], work[1]], axis=1)
    out_ref[...] = merged.reshape(16, 6, 16, 256).astype(BF)


def gather_groups(pieces):
    pieces = pieces + [jnp.zeros_like(pieces[0])]
    return jnp.concatenate(pieces, axis=1)


def time_kernel(*refs):
    count = len(PARTS) + 10
    sources, out_ref, targets = refs[:count], refs[count], refs[count + 1 : 2 * count + 1]
    work, held, rows, weight, arrival = refs[2 * count + 1 :]
    sources = list(sources)
    sources[0] = sources[0].at[:, :, pl.ds(0, 4864)]
    copies = start_copies(sources, targets, arrival)
    eye_ref, flip_ref, order_ref, forward_ref, inverse_ref, in_ref = targets[count - 6 :]
    for copy in copies[: count - 3]:
        copy.wait()
    own_weights(targets[0], eye_ref, weight, work)
    pair_weights(targets[1 : count - 6], flip_ref, order_ref, weight, work, held, rows)
    for copy in copies[count - 3 :]:
        copy.wait()

    def weighted(values, v):
        part = weight[v]
        return (values * jnp.concatenate([part, part], axis=0)).astype(BF)

    def forward(rows, n):
        return dot_table(forward_ref, rows, n)

    def inverse(rows, n):
        return dot_table(inverse_ref, rows, n)

    loaded = [in_ref[:, w].reshape(256, 256) for w in range(6)]
    for e in range(2):
        total = None
        for s in range(3):
            rows = gather_groups([loaded[2 * r + e][:, 64 * s : 64 * (s + 1)] for r in range(3)])
            term = forward(rows, 1 + s)
            total = term if total is None else total + term
        spectrum = weighted(total, 6 + e)
        tails = [inverse(spectrum, 1 + s) for s in range(3)]
        for r in range(3):
            w = 2 * r + e
            values = inverse(weighted(forward(loaded[w], 0), w), 0)
            values = values + gather_groups([tail[:, 64 * r : 64 * (r + 1)] for tail in tails])
            out_ref[:, w] = values.astype(BF).reshape(16, 16, 256)


def third_kernel(in_ref, table_ref, out_ref, work):
    values = in_ref[...].astype(F32).reshape(1536, 256)
    work[0] = values[:, :128]
    work[1] = values[:, 128:]

    def inverse(rows, n):
        return dot(table_ref[0, n], rows) + dot(table_ref[1, n], rows)

    def load(row):
        return get_rows(work, row, 192).astype(BF)

    for e in range(2):
        rows = load(6 + e)
        tails = [inverse(rows, 1 + s) for s in range(3)]
        for r in range(3):
            t = 2 * r + e
            values = inverse(load(t), 0)
            values = values + gather_groups([tail[:, 64 * r : 64 * (r + 1)] for tail in tails])
            out_ref[:, t] = values.astype(BF).reshape(8, 16, 256)


def last_kernel(
    info_ref, in_ref, tb_source, ta_source, sign_ref, own_ref, send_ref, work, spare, both,
    tb_ref, ta_ref, arrival
):
    copies = start_copies((tb_source, ta_source), (tb_ref, ta_ref), arrival)
    side = info_ref[2]
    values = in_ref[...].astype(F32).reshape(768, 256)
    work[0] = values[:, :128]
    work[1] = values[:, 128:]
    spare[...] = jnp.zeros_like(spare)
    for e in range(2):
        rows = get_rows(work, 6 + e, 96)
        spare[pl.ds(e, 96, stride=8), :] = rows[:, :128]
        spare[pl.ds(2 + e, 96, stride=8), :] = swap_half(rows[:, :128])
        spare[pl.ds(4 + e, 96, stride=8), :] = rows[:, 128:]
    low = low_half((48, 128))
    groups = [[] for _ in range(5)]
    shaped = values.reshape(8, 6, 2, 8, 256)
    shaped_spare = spare[...].reshape(8, 6, 2, 8, 128)
    for g in range(8):
        real_part = shaped[g, :, 0].reshape(48, 256)
        imag_part = shaped[g, :, 1].reshape(48, 256)
        for pair in range(2):
            real_tile = real_part[:, 128 * pair : 128 * (pair + 1)]
            imag_tile = imag_part[:, 128 * pair : 128 * (pair + 1)]
            groups[2 * pair].append(jnp.where(low, real_tile, swap_half(imag_tile)))
            groups[2 * pair + 1].append(jnp.where(low, swap_half(real_tile), imag_tile))
        real_tile = shaped_spare[g, :, 0].reshape(48, 128)
        imag_tile = shaped_spare[g, :, 1].reshape(48, 128)
        groups[4].append(jnp.where(low, real_tile, swap_half(imag_tile)))
    rows = jnp.concatenate([jnp.concatenate(group, axis=1) for group in groups], axis=0).astype(BF)
    for copy in copies:
        copy.wait()
    half = dot_columns(rows, tb_ref).astype(BF)
    rows = jnp.concatenate(
        [
            jnp.concatenate(
                [half[48 * ig : 48 * (ig + 1), 128 * y : 128 * (y + 1)] for ig in range(5)], axis=1
            )
            for y in range(6)
        ],
        axis=0,
    )
    result = dot_columns(rows, ta_ref) * sign_ref[...]
    for y in range(6):
        both[y // 3, :, 384 * (y % 3) : 384 * (y % 3 + 1)] = result[48 * y : 48 * (y + 1)]
    own = both[side]
    for t in range(6):
        own_ref[t] = own[8 * t : 8 * t + 6]
    send_ref[...] = both[1 - side].astype(BF)


def sum_kernel(own_ref, other_ref, out_ref):
    other = other_ref[...].astype(F32)
    for t in range(6):
        out_ref[t] = own_ref[t] + other[8 * t : 8 * t + 6]


def device_of(a, z, c):
    return (a * 8 + (z // 2) * 2 + c) * 2 + z % 2


def column_pairs(shift, flip):
    return [
        (device_of(a, (z + shift) % 8, c ^ flip), device_of(a, z, c))
        for a in range(16)
        for z in range(8)
        for c in range(2)
    ]


def mirror_pairs(a_from, g_from):
    return [
        ((((a_from - a) % 16) * 8 + (g_from - g) % 8) * 2 + 1 - h, (a * 8 + g) * 2 + h)
        for a in range(16)
        for g in range(8)
        for h in range(2)
    ]


def gather_column(block):
    def receive(values, shift, flip=0):
        return lax.ppermute(values, AXES, column_pairs(shift, flip))

    held = {0: block}
    for shift in (1, 7, 2, 6):
        held[shift] = receive(block, shift)
    held[3] = receive(held[2], 1)
    held[5] = receive(held[6], 7)
    held[4] = receive(held[2], 2)
    blocks = []
    for shift in SHIFTS:
        blocks += [held[shift], receive(held[shift], 0, 1)]
    return blocks


def shape(dims, dtype):
    return jax.ShapeDtypeStruct(dims, dtype)


def body(current, kernel):
    g = lax.axis_index("gz")
    h = lax.axis_index("gy")
    info = jnp.stack([(g // 2) * 2 + h, g % 2, h, g]).astype(jnp.int32)
    parity = jnp.arange(384) % 2
    sign = jnp.where((parity == 1) & (h == 1), -1.0, 1.0).astype(F32)
    flip, order, eye = mirror_tables()

    anywhere = pl.BlockSpec(memory_space=pl.ANY)
    block = call(raw_kernel, shape((48, 1152), BF), [pltpu.VMEM((48, 1152), F32)], vmem=8)(current)
    blocks = gather_column(block)

    line, corner = call(
        weight_line_kernel,
        [shape((24, 1152), BF), shape((8, 1152), BF)],
        [
            pltpu.VMEM((32, 1152), F32),
            pltpu.VMEM((6, 8, 4608), F32),
            pltpu.SemaphoreType.DMA,
        ],
        in_specs=[anywhere],
        vmem=59,
    )(kernel)
    line = lax.ppermute(line, AXES, mirror_pairs(15, 8))
    corner = lax.ppermute(corner, AXES, mirror_pairs(16, 8))
    sent = call(
        weight_send_kernel,
        [shape((n, 48, 1152), BF) for n in PARTS] + [shape((48, 1152), BF)],
        [
            pltpu.VMEM((48, 1152), F32),
            pltpu.VMEM((6, 12, 4608), F32),
            pltpu.SemaphoreType.DMA,
        ],
        in_specs=[anywhere] * 19,
        vmem=59,
    )(kernel, *blocks, line, corner)
    places = ((15, 7),) * len(PARTS) + ((16, 7),)
    arrived = [lax.ppermute(s, AXES, mirror_pairs(*place)) for s, place in zip(sent, places)]
    arrived += [line, corner]

    def spread(*operands):
        values = call(
            forward_kernel,
            shape((16, 6, 16, 256), BF),
            [
                pltpu.VMEM((6, 8, 48, 384), BF),
                pltpu.VMEM((6, 384, 640), BF),
                pltpu.VMEM((2, 1536, 128), F32),
                pltpu.VMEM((16, 48, 1152), BF),
                pltpu.VMEM((1, 384, 640), BF),
                pltpu.VMEM((768, 256), BF),
                pltpu.VMEM((2, 192, 128), BF),
                pltpu.SemaphoreType.DMA((19,)),
            ],
            in_specs=[smem_spec(), vmem_spec()] + [anywhere] * 19,
            vmem=59,
        )(*operands)
        return lax.all_to_all(values, "ta", split_axis=0, concat_axis=0, tiled=True)

    values = lax.cond(
        g < lax.axis_size("gz"),
        spread,
        lambda *operands: jnp.zeros((16, 6, 16, 256), BF),
        info, sign[None, :], *blocks, jnp.asarray(first_forward()), jnp.asarray(second_forward()),
        jnp.asarray(third_forward()),
    )
    operands = (
        kernel, *arrived, jnp.asarray(eye), jnp.asarray(flip), jnp.asarray(order),
        jnp.asarray(time_forward()), jnp.asarray(time_inverse()), values
    )
    values = call(
        time_kernel,
        shape((16, 6, 16, 256), BF),
        [pltpu.VMEM((6, 12, 4864), F32)]
        + [pltpu.VMEM(operand.shape, operand.dtype) for operand in operands[1:]]
        + [
            pltpu.VMEM((8, 256, 192), F32),
            pltpu.VMEM((48, 1152), F32),
            pltpu.VMEM((32, 1152), F32),
            pltpu.VMEM((8, 192, 256), F32),
            pltpu.SemaphoreType.DMA((len(operands),)),
        ],
        in_specs=[anywhere] * len(operands),
        vmem=59,
    )(*operands)
    values = lax.all_to_all(values, "ta", split_axis=0, concat_axis=0, tiled=True)
    values = call(third_kernel, shape((8, 6, 16, 256), BF), [pltpu.VMEM((2, 1536, 128), F32)])(
        values, jnp.asarray(third_inverse())
    )
    values = lax.all_to_all(values, "gz", split_axis=0, concat_axis=0, tiled=True)
    own, send = call(
        last_kernel,
        [shape((6, 6, 1152), F32), shape((48, 1152), BF)],
        [
            pltpu.VMEM((2, 768, 128), F32),
            pltpu.VMEM((768, 128), F32),
            pltpu.VMEM((2, 48, 1152), F32),
            pltpu.VMEM((1, 1024, 768), BF),
            pltpu.VMEM((2, 640, 384), BF),
            pltpu.SemaphoreType.DMA((2,)),
        ],
        in_specs=[smem_spec(), vmem_spec(), anywhere, anywhere, vmem_spec()],
    )(info, values, jnp.asarray(second_inverse()), jnp.asarray(first_inverse()), sign[None, :])
    other = lax.ppermute(send, "gy", [(0, 1), (1, 0)])
    return call(sum_kernel, shape((6, 6, 1152), F32), vmem=8)(own, other)


def solution(mesh):
    specs = P("ta", "gz", "gy")
    return jax.shard_map(
        body, mesh=mesh, in_specs=(specs, specs), out_specs=specs, check_vma=False
    )
```

```python
import numpy as np

import jax
import jax.numpy as jnp
from jax import lax
from jax.experimental import pallas as pl
from jax.experimental.pallas import tpu as pltpu
from jax.sharding import PartitionSpec as P


BF = jnp.bfloat16
F32 = jnp.float32
AXES = ("ta", "gz", "gy")
PARTS = (5,)
SHIFTS = (0, 1, 7, 2, 6, 3, 5, 4)


def split_table(table, parts=2):
    table = np.asarray(table, np.float32)
    upper = table.astype(jnp.bfloat16)
    if parts == 1:
        return upper[None]
    lower = (table - upper.astype(np.float32)).astype(jnp.bfloat16)
    return np.stack([upper, lower])


def turn(numerator, period, sign):
    angle = 2.0 * np.pi * (np.asarray(numerator) % period) / period
    cosine, sine = np.cos(angle), sign * np.sin(angle)
    return np.stack([np.stack([cosine, -sine]), np.stack([sine, cosine])])


def first_forward():
    x = np.arange(48)
    i = np.arange(25)
    parts = turn(x[:, None] * i[None, :], 96, -1.0)[:, 0]
    table = np.zeros((8, 48, 5, 128))
    for y in range(8):
        block = parts.reshape(2, 48, 5, 5).transpose(1, 2, 0, 3).reshape(48, 5, 10)
        table[y, :, :, y * 10 : y * 10 + 10] = block
    return split_table(table.reshape(384, 640), 1)


def second_forward():
    y = np.arange(48)
    out = np.zeros((8, 6, 128, 2, 64))
    for g in range(8):
        q = 12 * g + np.arange(12)
        parts = turn(y[:, None] * q[None, :], 96, -1.0)
        for i in range(5):
            for inp in range(2):
                for r in range(8):
                    out[g, :, r * 10 + inp * 5 + i, :, i * 12 : i * 12 + 12] = parts[
                        :, inp, r::8
                    ].transpose(1, 0, 2)
    table = split_table(out.reshape(8, 768, 128))
    return np.concatenate([table[0], table[1]], axis=2)


def third_forward():
    w = np.arange(96)
    z = np.arange(48)
    parts = turn(w[:, None] * z[None, :], 96, -1.0)
    table = np.zeros((96, 2, 2, 8, 8))
    table[..., :6] = parts.transpose(2, 0, 1, 3).reshape(96, 2, 2, 8, 6)
    return split_table(table.reshape(192, 128))


def time_forward():
    k = np.arange(192)
    t = np.arange(96)
    parts = turn(k[:, None] * t[None, :], 192, -1.0)
    parts = parts.transpose(0, 2, 3, 1).reshape(2, 192, 16, 6, 2).transpose(0, 1, 2, 4, 3)
    table = np.zeros((4, 2, 192, 16, 2, 8))
    table[0, ..., :6] = parts
    for s in range(3):
        table[1 + s, ..., 6:8] = parts[..., 2 * s : 2 * s + 2]
    return split_table(table.reshape(4, 384, 256), 1)


def time_inverse():
    k = np.arange(192)
    t = np.arange(96)
    parts = turn(t[:, None] * k[None, :], 192, 1.0) / 192.0
    parts = parts.reshape(2, 2, 16, 6, 192).transpose(2, 0, 3, 1, 4)
    table = np.zeros((4, 16, 2, 8, 2, 192))
    table[0, :, :, :6] = parts
    for s in range(3):
        table[1 + s, :, :, 6:8] = parts[:, :, 2 * s : 2 * s + 2]
    return split_table(table.reshape(4, 256, 384), 1)


def third_inverse():
    w = np.arange(96)
    z = np.arange(48)
    parts = turn(z[:, None] * w[None, :], 96, 1.0) / 96.0
    parts = parts.reshape(2, 2, 8, 6, 96).transpose(2, 0, 3, 4, 1)
    table = np.zeros((4, 8, 2, 8, 96, 2))
    table[0, :, :, :6] = parts
    for s in range(3):
        table[1 + s, :, :, 6:8] = parts[:, :, 2 * s : 2 * s + 2]
    return split_table(table.reshape(4, 128, 192))


def second_inverse():
    q = np.arange(96)
    y = np.arange(48)
    parts = turn(q[:, None] * y[None, :], 96, 1.0) / 96.0
    parts = parts.reshape(2, 2, 8, 12, 6, 8)
    table = np.zeros((8, 2, 64, 6, 128))
    for i in range(5):
        for r in range(8):
            for out in range(2):
                table[:, :, i * 12 : i * 12 + 12, :, r * 10 + out * 5 + i] = parts[
                    out, :, :, :, :, r
                ].transpose(1, 0, 2, 3)
    return split_table(table.reshape(1024, 768), 1)


def first_inverse():
    i = np.arange(25)
    x = np.arange(48)
    parts = turn(i[:, None] * x[None, :], 96, 1.0)[0] / 96.0
    table = np.zeros((5, 128, 8, 48))
    for r in range(8):
        for inp in range(2):
            table[:, r * 10 + inp * 5 : r * 10 + inp * 5 + 5, r] = parts[inp].reshape(5, 5, 48)
    return split_table(table.reshape(640, 384))


def mirror_tables():
    flip = np.zeros((192, 192))
    flip[np.arange(192), (-np.arange(192)) % 192] = 1.0
    order = np.zeros((256, 256))
    for group in range(4):
        for i in range(5):
            for q in range(12):
                row = group * 64 + i * 12
                order[row + q, row + (12 - q) % 12] = 1.0
    return flip.astype(jnp.bfloat16), order.astype(jnp.bfloat16), np.eye(192).astype(jnp.bfloat16)


def dot(left, right):
    return lax.dot_general(left, right, (((1,), (0,)), ((), ())), preferred_element_type=F32)


def dot_table(table_ref, rows, *place):
    total = dot(table_ref[(0, *place)], rows)
    for n in range(1, table_ref.shape[0]):
        total = total + dot(table_ref[(n, *place)], rows)
    return total


def dot_columns(rows, table_ref):
    total = dot(rows, table_ref[0])
    for n in range(1, table_ref.shape[0]):
        total = total + dot(rows, table_ref[n])
    return total


def start_copies(sources, targets, arrival):
    copies = [
        pltpu.make_async_copy(source, target, arrival.at[n])
        for n, (source, target) in enumerate(zip(sources, targets))
    ]
    for copy in copies:
        copy.start()
    return copies


def dot_rows(left, right):
    return lax.dot_general(left, right, (((1,), (1,)), ((), ())), preferred_element_type=F32)


def low_half(shape):
    return lax.broadcasted_iota(jnp.int32, shape, 1) % 128 < 64


def swap_half(values):
    return pltpu.roll(values, 64, 1)


def call(kernel, out_shape, scratch=(), in_specs=None, grid=(), vmem=14, flops=10**8, moved=4 * 10**6):
    placed = {} if in_specs is None else {"in_specs": in_specs}
    return pl.pallas_call(
        kernel,
        out_shape=out_shape,
        **placed,
        grid=grid,
        scratch_shapes=list(scratch),
        compiler_params=pltpu.CompilerParams(vmem_limit_bytes=vmem * 2**20),
        cost_estimate=pl.CostEstimate(flops=flops, bytes_accessed=moved, transcendentals=0),
    )


def vmem_spec():
    return pl.BlockSpec(memory_space=pltpu.VMEM)


def smem_spec():
    return pl.BlockSpec(memory_space=pltpu.SMEM)


def raw_kernel(current_ref, out_ref, work):
    work[...] = jnp.zeros_like(work)
    for t in range(6):
        work[8 * t : 8 * t + 6, :] = current_ref[t]
    out_ref[...] = work[...].astype(BF)


def part_of(plane):
    for part, count in enumerate(PARTS):
        if plane < count:
            return part, plane
        plane -= count


def weight_send_kernel(source_ref, *refs):
    refs = refs[16:]
    plane_ref, line_ref, corner_ref, work, rows, kernel_ref, arrival = refs[len(PARTS) :]
    copy = pltpu.make_async_copy(source_ref.at[:, :, pl.ds(4608, 4608)], kernel_ref, arrival)
    copy.start()
    copy.wait()
    rows[...] = jnp.zeros_like(rows)
    for w in range(6):
        for c in range(4):
            piece = kernel_ref[w, :, 1152 * c : 1152 * (c + 1)]
            work[12 * c : 12 * c + 12, :] = piece
            rows[4 * w + c : 4 * w + c + 1, :] = piece[0:1]
        if w == 0:
            plane_ref[...] = work[...].astype(BF)
        else:
            part, place = part_of(w - 1)
            refs[part][place] = work[...].astype(BF)
    line_ref[...] = rows[4:28, :].astype(BF)
    corner_ref[...] = rows[0:8, :].astype(BF)


def own_weights(kernel_ref, eye_ref, weight, work):
    eye = eye_ref[...]
    work[...] = jnp.zeros_like(work)
    for w in range(6):
        for i in range(25):
            piece = kernel_ref[w, :, 192 * i : 192 * (i + 1)]
            row = 64 * (i // 5) + 12 * (i % 5)
            if i < 20:
                work[w, row : row + 12, :] = piece
            else:
                row = 64 * (w // 2) + 12 * (i % 5)
                work[6 + w % 2, row : row + 12, :] = piece
    for v in range(8):
        values = work[v]
        upper = values.astype(BF)
        lower = (values - upper.astype(F32)).astype(BF)
        weight[v] = dot_rows(eye, upper) + dot_rows(eye, lower)


def pair_weights(refs, flip_ref, order_ref, weight, work, held, rows):
    plane_ref, line_ref, corner_ref = refs[len(PARTS) :]
    flip, order = flip_ref[...], order_ref[...]
    work[...] = jnp.zeros_like(work)
    rows[0:8, :] = corner_ref[...].astype(F32)
    rows[8:32, :] = line_ref[...].astype(F32)
    for w in range(6):
        if w == 0:
            held[...] = plane_ref[...].astype(F32)
            first = 0
        else:
            part, place = part_of(5 - w)
            held[...] = refs[part][place].astype(F32)
            first = 8 + 4 * (5 - w)
        for i in range(1, 24):
            c, p = (24 - i) // 6, (24 - i) % 6
            piece = held[12 * c : 12 * c + 12, 192 * p : 192 * (p + 1)]
            line = rows[first + c : first + c + 1, 192 * p : 192 * (p + 1)]
            if i < 20:
                v, row = w, 64 * (i // 5) + 12 * (i % 5)
            else:
                v, row = 6 + w % 2, 64 * (w // 2) + 12 * (i % 5)
            work[v, row : row + 12, :] = piece
            work[v, row : row + 1, :] = line
    for v in range(8):
        turned = dot(order, work[v].astype(BF)).astype(BF)
        weight[v] = weight[v] + dot_rows(flip, turned)


def put_rows(work, row, count, values):
    work[0, pl.ds(row, count, stride=8), :] = values[:, :128]
    work[1, pl.ds(row, count, stride=8), :] = values[:, 128:]


def get_rows(work, row, count):
    halves = [work[n, pl.ds(row, count, stride=8), :] for n in range(2)]
    return jnp.concatenate(halves, axis=1)


def forward_kernel(info_ref, sign_ref, *refs):
    sources = list(refs[:19])
    sources[17] = sources[17].at[info_ref[3]]
    out_ref, raw, half, work, blocks, ta_ref, tb_ref, t3_ref, arrival = refs[19:]
    targets = [blocks.at[n] for n in range(16)] + [ta_ref, tb_ref, t3_ref]
    copies = start_copies(sources, targets, arrival)
    for copy in copies[:17]:
        copy.wait()
    place, core = info_ref[0], info_ref[1]
    for n in range(16):
        spot = lax.rem(place + SHIFTS[n // 2], 8)
        side = lax.rem(spot, 2)
        plane = (spot // 2) * 2 + (core if n % 2 == 0 else 1 - core)
        for y in range(3):
            raw[side * 3 + y, plane] = blocks[n, :, 384 * y : 384 * (y + 1)]
    for y in range(6):
        rows = raw[y].reshape(384, 384)
        half[y] = dot_columns(rows * sign_ref[...], ta_ref).astype(BF)
    for copy in copies[17:]:
        copy.wait()
    seconds = []
    for ig in range(5):
        merged = jnp.concatenate([half[y, :, 128 * ig : 128 * (ig + 1)] for y in range(6)], axis=1)
        both = dot(merged, tb_ref[...])
        seconds.append(both[:, :128] + both[:, 128:])
    low = low_half((384, 128))
    real_main, imag_main = [], []
    for pair in range(2):
        left, right = seconds[2 * pair], seconds[2 * pair + 1]
        real_main.append(jnp.where(low, left, swap_half(right)))
        imag_main.append(jnp.where(low, swap_half(left), right))
    real_main = jnp.concatenate(real_main, axis=1).reshape(8, 6, 8, 256)
    imag_main = jnp.concatenate(imag_main, axis=1).reshape(8, 6, 8, 256)
    last = seconds[4].reshape(8, 6, 8, 128)
    turned = swap_half(seconds[4]).reshape(8, 6, 8, 128)
    low = low_half((64, 128))

    def finish(row, real_part, imag_part):
        merged = jnp.concatenate([real_part, imag_part], axis=0).astype(BF)
        put_rows(work, row, 192, dot_table(t3_ref, merged))

    for t in range(6):
        finish(t, real_main[:, t].reshape(64, 256), imag_main[:, t].reshape(64, 256))
    for e in range(2):
        plain = [last[:, e + 2 * s].reshape(64, 128) for s in range(3)]
        moved = [turned[:, e + 2 * s].reshape(64, 128) for s in range(3)]
        real_part = [jnp.where(low, plain[0], moved[1]), jnp.where(low, plain[2], 0.0)]
        imag_part = [jnp.where(low, moved[0], plain[1]), jnp.where(low, moved[2], 0.0)]
        finish(6 + e, jnp.concatenate(real_part, axis=1), jnp.concatenate(imag_part, axis=1))
    merged = jnp.concatenate([work[0], work[1]], axis=1)
    out_ref[...] = merged.reshape(16, 6, 16, 256).astype(BF)


def gather_groups(pieces):
    pieces = pieces + [jnp.zeros_like(pieces[0])]
    return jnp.concatenate(pieces, axis=1)


def time_kernel(*refs):
    count = len(PARTS) + 10
    sources, out_ref, targets = refs[:count], refs[count], refs[count + 1 : 2 * count + 1]
    work, held, rows, weight, arrival = refs[2 * count + 1 :]
    sources = list(sources)
    sources[0] = sources[0].at[:, :, pl.ds(0, 4864)]
    copies = start_copies(sources, targets, arrival)
    eye_ref, flip_ref, order_ref, forward_ref, inverse_ref, in_ref = targets[count - 6 :]
    copies[0].wait()
    copies[count - 6].wait()
    own_weights(targets[0], eye_ref, weight, work)
    for copy in copies[1 : count - 6] + copies[count - 5 : count - 3]:
        copy.wait()
    pair_weights(targets[1 : count - 6], flip_ref, order_ref, weight, work, held, rows)
    for copy in copies[count - 3 :]:
        copy.wait()

    def weighted(values, v):
        part = weight[v]
        return (values * jnp.concatenate([part, part], axis=0)).astype(BF)

    def forward(rows, n):
        return dot_table(forward_ref, rows, n)

    def inverse(rows, n):
        return dot_table(inverse_ref, rows, n)

    loaded = [in_ref[:, w].reshape(256, 256) for w in range(6)]
    for e in range(2):
        total = None
        for s in range(3):
            rows = gather_groups([loaded[2 * r + e][:, 64 * s : 64 * (s + 1)] for r in range(3)])
            term = forward(rows, 1 + s)
            total = term if total is None else total + term
        spectrum = weighted(total, 6 + e)
        tails = [inverse(spectrum, 1 + s) for s in range(3)]
        for r in range(3):
            w = 2 * r + e
            values = inverse(weighted(forward(loaded[w], 0), w), 0)
            values = values + gather_groups([tail[:, 64 * r : 64 * (r + 1)] for tail in tails])
            out_ref[:, w] = values.astype(BF).reshape(16, 16, 256)


def third_kernel(in_ref, table_ref, out_ref, work):
    values = in_ref[...].astype(F32).reshape(1536, 256)
    work[0] = values[:, :128]
    work[1] = values[:, 128:]

    def inverse(rows, n):
        return dot(table_ref[0, n], rows) + dot(table_ref[1, n], rows)

    def load(row):
        return get_rows(work, row, 192).astype(BF)

    for e in range(2):
        rows = load(6 + e)
        tails = [inverse(rows, 1 + s) for s in range(3)]
        for r in range(3):
            t = 2 * r + e
            values = inverse(load(t), 0)
            values = values + gather_groups([tail[:, 64 * r : 64 * (r + 1)] for tail in tails])
            out_ref[:, t] = values.astype(BF).reshape(8, 16, 256)


def last_kernel(
    info_ref, in_ref, tb_source, ta_source, sign_ref, own_ref, send_ref, work, spare, both,
    tb_ref, ta_ref, arrival
):
    copies = start_copies((tb_source, ta_source), (tb_ref, ta_ref), arrival)
    side = info_ref[2]
    values = in_ref[...].astype(F32).reshape(768, 256)
    work[0] = values[:, :128]
    work[1] = values[:, 128:]
    spare[...] = jnp.zeros_like(spare)
    for e in range(2):
        rows = get_rows(work, 6 + e, 96)
        spare[pl.ds(e, 96, stride=8), :] = rows[:, :128]
        spare[pl.ds(2 + e, 96, stride=8), :] = swap_half(rows[:, :128])
        spare[pl.ds(4 + e, 96, stride=8), :] = rows[:, 128:]
    low = low_half((48, 128))
    groups = [[] for _ in range(5)]
    shaped = values.reshape(8, 6, 2, 8, 256)
    shaped_spare = spare[...].reshape(8, 6, 2, 8, 128)
    for g in range(8):
        real_part = shaped[g, :, 0].reshape(48, 256)
        imag_part = shaped[g, :, 1].reshape(48, 256)
        for pair in range(2):
            real_tile = real_part[:, 128 * pair : 128 * (pair + 1)]
            imag_tile = imag_part[:, 128 * pair : 128 * (pair + 1)]
            groups[2 * pair].append(jnp.where(low, real_tile, swap_half(imag_tile)))
            groups[2 * pair + 1].append(jnp.where(low, swap_half(real_tile), imag_tile))
        real_tile = shaped_spare[g, :, 0].reshape(48, 128)
        imag_tile = shaped_spare[g, :, 1].reshape(48, 128)
        groups[4].append(jnp.where(low, real_tile, swap_half(imag_tile)))
    rows = jnp.concatenate([jnp.concatenate(group, axis=1) for group in groups], axis=0).astype(BF)
    for copy in copies:
        copy.wait()
    half = dot_columns(rows, tb_ref).astype(BF)
    rows = jnp.concatenate(
        [
            jnp.concatenate(
                [half[48 * ig : 48 * (ig + 1), 128 * y : 128 * (y + 1)] for ig in range(5)], axis=1
            )
            for y in range(6)
        ],
        axis=0,
    )
    result = dot_columns(rows, ta_ref) * sign_ref[...]
    for y in range(6):
        both[y // 3, :, 384 * (y % 3) : 384 * (y % 3 + 1)] = result[48 * y : 48 * (y + 1)]
    own = both[side]
    for t in range(6):
        own_ref[t] = own[8 * t : 8 * t + 6]
    send_ref[...] = both[1 - side].astype(BF)


def sum_kernel(own_ref, other_ref, out_ref):
    other = other_ref[...].astype(F32)
    for t in range(6):
        out_ref[t] = own_ref[t] + other[8 * t : 8 * t + 6]


def device_of(a, z, c):
    return (a * 8 + (z // 2) * 2 + c) * 2 + z % 2


def column_pairs(shift, flip):
    return [
        (device_of(a, (z + shift) % 8, c ^ flip), device_of(a, z, c))
        for a in range(16)
        for z in range(8)
        for c in range(2)
    ]


def mirror_pairs(a_from, g_from):
    return [
        ((((a_from - a) % 16) * 8 + (g_from - g) % 8) * 2 + 1 - h, (a * 8 + g) * 2 + h)
        for a in range(16)
        for g in range(8)
        for h in range(2)
    ]


def gather_column(block):
    def receive(values, shift, flip=0):
        return lax.ppermute(values, AXES, column_pairs(shift, flip))

    held = {0: block}
    for shift in (1, 7, 2, 6):
        held[shift] = receive(block, shift)
    held[3] = receive(held[2], 1)
    held[5] = receive(held[6], 7)
    held[4] = receive(held[2], 2)
    blocks = []
    for shift in SHIFTS:
        blocks += [held[shift], receive(held[shift], 0, 1)]
    return blocks


def shape(dims, dtype):
    return jax.ShapeDtypeStruct(dims, dtype)


def body(current, kernel):
    g = lax.axis_index("gz")
    h = lax.axis_index("gy")
    info = jnp.stack([(g // 2) * 2 + h, g % 2, h, g]).astype(jnp.int32)
    parity = jnp.arange(384) % 2
    sign = jnp.where((parity == 1) & (h == 1), -1.0, 1.0).astype(F32)
    flip, order, eye = mirror_tables()

    anywhere = pl.BlockSpec(memory_space=pl.ANY)
    block = call(raw_kernel, shape((48, 1152), BF), [pltpu.VMEM((48, 1152), F32)], vmem=8)(current)
    blocks = gather_column(block)

    sent = call(
        weight_send_kernel,
        [shape((n, 48, 1152), BF) for n in PARTS]
        + [shape((48, 1152), BF), shape((24, 1152), BF), shape((8, 1152), BF)],
        [pltpu.VMEM((48, 1152), F32), pltpu.VMEM((32, 1152), F32)]
        + [pltpu.VMEM((6, 12, 4608), F32), pltpu.SemaphoreType.DMA],
        in_specs=[anywhere] * 17,
        vmem=59,
    )(kernel, *blocks)
    places = ((15, 7),) * len(PARTS) + ((16, 7), (15, 8), (16, 8))
    arrived = [lax.ppermute(s, AXES, mirror_pairs(*place)) for s, place in zip(sent, places)]
    def spread(*operands):
        values = call(
            forward_kernel,
            shape((16, 6, 16, 256), BF),
            [
                pltpu.VMEM((6, 8, 48, 384), BF),
                pltpu.VMEM((6, 384, 640), BF),
                pltpu.VMEM((2, 1536, 128), F32),
                pltpu.VMEM((16, 48, 1152), BF),
                pltpu.VMEM((1, 384, 640), BF),
                pltpu.VMEM((768, 256), BF),
                pltpu.VMEM((2, 192, 128), BF),
                pltpu.SemaphoreType.DMA((19,)),
            ],
            in_specs=[smem_spec(), vmem_spec()] + [anywhere] * 19,
            vmem=59,
        )(*operands)
        return lax.all_to_all(values, "ta", split_axis=0, concat_axis=0, tiled=True)

    values = lax.cond(
        g < lax.axis_size("gz"),
        spread,
        lambda *operands: jnp.zeros((16, 6, 16, 256), BF),
        info, sign[None, :].astype(BF), *blocks, jnp.asarray(first_forward()), jnp.asarray(second_forward()),
        jnp.asarray(third_forward()),
    )
    operands = (
        kernel, *arrived, jnp.asarray(eye), jnp.asarray(flip), jnp.asarray(order),
        jnp.asarray(time_forward()), jnp.asarray(time_inverse()), values
    )
    values = call(
        time_kernel,
        shape((16, 6, 16, 256), BF),
        [pltpu.VMEM((6, 12, 4864), F32)]
        + [pltpu.VMEM(operand.shape, operand.dtype) for operand in operands[1:]]
        + [
            pltpu.VMEM((8, 256, 192), F32),
            pltpu.VMEM((48, 1152), F32),
            pltpu.VMEM((32, 1152), F32),
            pltpu.VMEM((8, 192, 256), F32),
            pltpu.SemaphoreType.DMA((len(operands),)),
        ],
        in_specs=[anywhere] * len(operands),
        vmem=59,
    )(*operands)
    values = lax.all_to_all(values, "ta", split_axis=0, concat_axis=0, tiled=True)
    values = call(third_kernel, shape((8, 6, 16, 256), BF), [pltpu.VMEM((2, 1536, 128), F32)])(
        values, jnp.asarray(third_inverse())
    )
    values = lax.all_to_all(values, "gz", split_axis=0, concat_axis=0, tiled=True)
    own, send = call(
        last_kernel,
        [shape((6, 6, 1152), F32), shape((48, 1152), BF)],
        [
            pltpu.VMEM((2, 768, 128), F32),
            pltpu.VMEM((768, 128), F32),
            pltpu.VMEM((2, 48, 1152), F32),
            pltpu.VMEM((1, 1024, 768), BF),
            pltpu.VMEM((2, 640, 384), BF),
            pltpu.SemaphoreType.DMA((2,)),
        ],
        in_specs=[smem_spec(), vmem_spec(), anywhere, anywhere, vmem_spec()],
    )(info, values, jnp.asarray(second_inverse()), jnp.asarray(first_inverse()), sign[None, :])
    other = lax.ppermute(send, "gy", [(0, 1), (1, 0)])
    return call(sum_kernel, shape((6, 6, 1152), F32), vmem=8)(own, other)


def solution(mesh):
    specs = P("ta", "gz", "gy")
    return jax.shard_map(
        body, mesh=mesh, in_specs=(specs, specs), out_specs=specs, check_vma=False
    )
```

```python
import numpy as np

import jax
import jax.numpy as jnp
from jax import lax
from jax.experimental import pallas as pl
from jax.experimental.pallas import tpu as pltpu
from jax.sharding import PartitionSpec as P


BF = jnp.bfloat16
F32 = jnp.float32
AXES = ("ta", "gz", "gy")
PARTS = (5,)
SHIFTS = (0, 1, 7, 2, 6, 3, 5, 4)


def split_table(table, parts=2):
    table = np.asarray(table, np.float32)
    upper = table.astype(jnp.bfloat16)
    if parts == 1:
        return upper[None]
    lower = (table - upper.astype(np.float32)).astype(jnp.bfloat16)
    return np.stack([upper, lower])


def turn(numerator, period, sign):
    angle = 2.0 * np.pi * (np.asarray(numerator) % period) / period
    cosine, sine = np.cos(angle), sign * np.sin(angle)
    return np.stack([np.stack([cosine, -sine]), np.stack([sine, cosine])])


def first_forward():
    x = np.arange(48)
    i = np.arange(25)
    parts = turn(x[:, None] * i[None, :], 96, -1.0)[:, 0]
    table = np.zeros((8, 48, 5, 128))
    for y in range(8):
        block = parts.reshape(2, 48, 5, 5).transpose(1, 2, 0, 3).reshape(48, 5, 10)
        table[y, :, :, y * 10 : y * 10 + 10] = block
    return split_table(table.reshape(384, 640), 1)


def second_forward():
    y = np.arange(48)
    out = np.zeros((8, 6, 128, 2, 64))
    for g in range(8):
        q = 12 * g + np.arange(12)
        parts = turn(y[:, None] * q[None, :], 96, -1.0)
        for i in range(5):
            for inp in range(2):
                for r in range(8):
                    out[g, :, r * 10 + inp * 5 + i, :, i * 12 : i * 12 + 12] = parts[
                        :, inp, r::8
                    ].transpose(1, 0, 2)
    table = split_table(out.reshape(8, 768, 128))
    return np.concatenate([table[0], table[1]], axis=2)


def third_forward():
    w = np.arange(96)
    z = np.arange(48)
    parts = turn(w[:, None] * z[None, :], 96, -1.0)
    table = np.zeros((96, 2, 2, 8, 8))
    table[..., :6] = parts.transpose(2, 0, 1, 3).reshape(96, 2, 2, 8, 6)
    return split_table(table.reshape(192, 128))


def time_forward():
    k = np.arange(192)
    t = np.arange(96)
    parts = turn(k[:, None] * t[None, :], 192, -1.0)
    parts = parts.transpose(0, 2, 3, 1).reshape(2, 192, 16, 6, 2).transpose(0, 1, 2, 4, 3)
    table = np.zeros((4, 2, 192, 16, 2, 8))
    table[0, ..., :6] = parts
    for s in range(3):
        table[1 + s, ..., 6:8] = parts[..., 2 * s : 2 * s + 2]
    return split_table(table.reshape(4, 384, 256), 1)


def time_inverse():
    k = np.arange(192)
    t = np.arange(96)
    parts = turn(t[:, None] * k[None, :], 192, 1.0) / 192.0
    parts = parts.reshape(2, 2, 16, 6, 192).transpose(2, 0, 3, 1, 4)
    table = np.zeros((4, 16, 2, 8, 2, 192))
    table[0, :, :, :6] = parts
    for s in range(3):
        table[1 + s, :, :, 6:8] = parts[:, :, 2 * s : 2 * s + 2]
    return split_table(table.reshape(4, 256, 384), 1)


def third_inverse():
    w = np.arange(96)
    z = np.arange(48)
    parts = turn(z[:, None] * w[None, :], 96, 1.0) / 96.0
    parts = parts.reshape(2, 2, 8, 6, 96).transpose(2, 0, 3, 4, 1)
    table = np.zeros((4, 8, 2, 8, 96, 2))
    table[0, :, :, :6] = parts
    for s in range(3):
        table[1 + s, :, :, 6:8] = parts[:, :, 2 * s : 2 * s + 2]
    return split_table(table.reshape(4, 128, 192))


def second_inverse():
    q = np.arange(96)
    y = np.arange(48)
    parts = turn(q[:, None] * y[None, :], 96, 1.0) / 96.0
    parts = parts.reshape(2, 2, 8, 12, 6, 8)
    table = np.zeros((8, 2, 64, 6, 128))
    for i in range(5):
        for r in range(8):
            for out in range(2):
                table[:, :, i * 12 : i * 12 + 12, :, r * 10 + out * 5 + i] = parts[
                    out, :, :, :, :, r
                ].transpose(1, 0, 2, 3)
    return split_table(table.reshape(1024, 768), 1)


def first_inverse():
    i = np.arange(25)
    x = np.arange(48)
    parts = turn(i[:, None] * x[None, :], 96, 1.0)[0] / 96.0
    table = np.zeros((5, 128, 8, 48))
    for r in range(8):
        for inp in range(2):
            table[:, r * 10 + inp * 5 : r * 10 + inp * 5 + 5, r] = parts[inp].reshape(5, 5, 48)
    return split_table(table.reshape(640, 384))


def mirror_tables():
    flip = np.zeros((192, 192))
    flip[np.arange(192), (-np.arange(192)) % 192] = 1.0
    order = np.zeros((256, 256))
    for group in range(4):
        for i in range(5):
            for q in range(12):
                row = group * 64 + i * 12
                order[row + q, row + (12 - q) % 12] = 1.0
    return flip.astype(jnp.bfloat16), order.astype(jnp.bfloat16), np.eye(192).astype(jnp.bfloat16)


def dot(left, right):
    return lax.dot_general(left, right, (((1,), (0,)), ((), ())), preferred_element_type=F32)


def dot_table(table_ref, rows, *place):
    total = dot(table_ref[(0, *place)], rows)
    for n in range(1, table_ref.shape[0]):
        total = total + dot(table_ref[(n, *place)], rows)
    return total


def dot_columns(rows, table_ref):
    total = dot(rows, table_ref[0])
    for n in range(1, table_ref.shape[0]):
        total = total + dot(rows, table_ref[n])
    return total


def start_copies(sources, targets, arrival):
    copies = [
        pltpu.make_async_copy(source, target, arrival.at[n])
        for n, (source, target) in enumerate(zip(sources, targets))
    ]
    for copy in copies:
        copy.start()
    return copies


def dot_rows(left, right):
    return lax.dot_general(left, right, (((1,), (1,)), ((), ())), preferred_element_type=F32)


def low_half(shape):
    return lax.broadcasted_iota(jnp.int32, shape, 1) % 128 < 64


def swap_half(values):
    return pltpu.roll(values, 64, 1)


def call(kernel, out_shape, scratch=(), in_specs=None, grid=(), vmem=14, flops=10**8, moved=4 * 10**6):
    placed = {} if in_specs is None else {"in_specs": in_specs}
    return pl.pallas_call(
        kernel,
        out_shape=out_shape,
        **placed,
        grid=grid,
        scratch_shapes=list(scratch),
        compiler_params=pltpu.CompilerParams(vmem_limit_bytes=vmem * 2**20),
        cost_estimate=pl.CostEstimate(flops=flops, bytes_accessed=moved, transcendentals=0),
    )


def vmem_spec():
    return pl.BlockSpec(memory_space=pltpu.VMEM)


def smem_spec():
    return pl.BlockSpec(memory_space=pltpu.SMEM)


def raw_kernel(current_ref, out_ref, work):
    work[...] = jnp.zeros_like(work)
    for t in range(6):
        work[8 * t : 8 * t + 6, :] = current_ref[t]
    out_ref[...] = work[...].astype(BF)


def part_of(plane):
    for part, count in enumerate(PARTS):
        if plane < count:
            return part, plane
        plane -= count


def weight_send_kernel(source_ref, *refs):
    refs = refs[16:]
    plane_ref, line_ref, corner_ref, work, rows, kernel_ref, arrival = refs[len(PARTS) :]
    copy = pltpu.make_async_copy(source_ref.at[:, :, pl.ds(4608, 4608)], kernel_ref, arrival)
    copy.start()
    copy.wait()
    rows[...] = jnp.zeros_like(rows)
    for w in range(6):
        for c in range(4):
            piece = kernel_ref[w, :, 1152 * c : 1152 * (c + 1)]
            work[12 * c : 12 * c + 12, :] = piece
            rows[4 * w + c : 4 * w + c + 1, :] = piece[0:1]
        if w == 0:
            plane_ref[...] = work[...].astype(BF)
        else:
            part, place = part_of(w - 1)
            refs[part][place] = work[...].astype(BF)
    line_ref[...] = rows[4:28, :].astype(BF)
    corner_ref[...] = rows[0:8, :].astype(BF)


def own_weights(kernel_ref, eye_ref, weight, work):
    eye = eye_ref[...]
    work[...] = jnp.zeros_like(work)
    for w in range(6):
        for i in range(25):
            piece = kernel_ref[w, :, 192 * i : 192 * (i + 1)]
            row = 64 * (i // 5) + 12 * (i % 5)
            if i < 20:
                work[w, row : row + 12, :] = piece
            else:
                row = 64 * (w // 2) + 12 * (i % 5)
                work[6 + w % 2, row : row + 12, :] = piece
    for v in range(8):
        values = work[v]
        upper = values.astype(BF)
        lower = (values - upper.astype(F32)).astype(BF)
        weight[v] = dot_rows(eye, upper) + dot_rows(eye, lower)


def pair_weights(refs, flip_ref, order_ref, weight, work, held, rows):
    plane_ref, line_ref, corner_ref = refs[len(PARTS) :]
    flip, order = flip_ref[...], order_ref[...]
    work[...] = jnp.zeros_like(work)
    rows[0:8, :] = corner_ref[...].astype(F32)
    rows[8:32, :] = line_ref[...].astype(F32)
    for w in range(6):
        if w == 0:
            held[...] = plane_ref[...].astype(F32)
            first = 0
        else:
            part, place = part_of(5 - w)
            held[...] = refs[part][place].astype(F32)
            first = 8 + 4 * (5 - w)
        for i in range(1, 24):
            c, p = (24 - i) // 6, (24 - i) % 6
            piece = held[12 * c : 12 * c + 12, 192 * p : 192 * (p + 1)]
            line = rows[first + c : first + c + 1, 192 * p : 192 * (p + 1)]
            if i < 20:
                v, row = w, 64 * (i // 5) + 12 * (i % 5)
            else:
                v, row = 6 + w % 2, 64 * (w // 2) + 12 * (i % 5)
            work[v, row : row + 12, :] = piece
            work[v, row : row + 1, :] = line
    for v in range(8):
        turned = dot(order, work[v].astype(BF)).astype(BF)
        weight[v] = weight[v] + dot_rows(flip, turned)


def put_rows(work, row, count, values):
    work[0, pl.ds(row, count, stride=8), :] = values[:, :128]
    work[1, pl.ds(row, count, stride=8), :] = values[:, 128:]


def get_rows(work, row, count):
    halves = [work[n, pl.ds(row, count, stride=8), :] for n in range(2)]
    return jnp.concatenate(halves, axis=1)


def forward_kernel(info_ref, sign_ref, *refs):
    sources = list(refs[:19])
    sources[17] = sources[17].at[info_ref[3]]
    out_ref, raw, half, work, blocks, ta_ref, tb_ref, t3_ref, arrival = refs[19:]
    targets = [blocks.at[n] for n in range(16)] + [ta_ref, tb_ref, t3_ref]
    copies = start_copies(sources, targets, arrival)
    for copy in copies[:17]:
        copy.wait()
    place, core = info_ref[0], info_ref[1]
    for n in range(16):
        spot = lax.rem(place + SHIFTS[n // 2], 8)
        side = lax.rem(spot, 2)
        plane = (spot // 2) * 2 + (core if n % 2 == 0 else 1 - core)
        for y in range(3):
            raw[side * 3 + y, plane] = blocks[n, :, 384 * y : 384 * (y + 1)]
    for y in range(6):
        rows = raw[y].reshape(384, 384)
        rows = (rows.astype(F32) * sign_ref[...]).astype(BF)
        half[y] = dot_columns(rows, ta_ref).astype(BF)
    for copy in copies[17:]:
        copy.wait()
    seconds = []
    for ig in range(5):
        merged = jnp.concatenate([half[y, :, 128 * ig : 128 * (ig + 1)] for y in range(6)], axis=1)
        both = dot(merged, tb_ref[...])
        seconds.append(both[:, :128] + both[:, 128:])
    low = low_half((384, 128))
    real_main, imag_main = [], []
    for pair in range(2):
        left, right = seconds[2 * pair], seconds[2 * pair + 1]
        real_main.append(jnp.where(low, left, swap_half(right)))
        imag_main.append(jnp.where(low, swap_half(left), right))
    real_main = jnp.concatenate(real_main, axis=1).reshape(8, 6, 8, 256)
    imag_main = jnp.concatenate(imag_main, axis=1).reshape(8, 6, 8, 256)
    last = seconds[4].reshape(8, 6, 8, 128)
    turned = swap_half(seconds[4]).reshape(8, 6, 8, 128)
    low = low_half((64, 128))

    def finish(row, real_part, imag_part):
        merged = jnp.concatenate([real_part, imag_part], axis=0).astype(BF)
        put_rows(work, row, 192, dot_table(t3_ref, merged))

    for t in range(6):
        finish(t, real_main[:, t].reshape(64, 256), imag_main[:, t].reshape(64, 256))
    for e in range(2):
        plain = [last[:, e + 2 * s].reshape(64, 128) for s in range(3)]
        moved = [turned[:, e + 2 * s].reshape(64, 128) for s in range(3)]
        real_part = [jnp.where(low, plain[0], moved[1]), jnp.where(low, plain[2], 0.0)]
        imag_part = [jnp.where(low, moved[0], plain[1]), jnp.where(low, moved[2], 0.0)]
        finish(6 + e, jnp.concatenate(real_part, axis=1), jnp.concatenate(imag_part, axis=1))
    merged = jnp.concatenate([work[0], work[1]], axis=1)
    out_ref[...] = merged.reshape(16, 6, 16, 256).astype(BF)


def gather_groups(pieces):
    pieces = pieces + [jnp.zeros_like(pieces[0])]
    return jnp.concatenate(pieces, axis=1)


def time_kernel(*refs):
    count = len(PARTS) + 10
    sources, out_ref, targets = refs[:count], refs[count], refs[count + 1 : 2 * count + 1]
    work, held, rows, weight, arrival = refs[2 * count + 1 :]
    sources = list(sources)
    sources[0] = sources[0].at[:, :, pl.ds(0, 4864)]
    copies = start_copies(sources, targets, arrival)
    eye_ref, flip_ref, order_ref, forward_ref, inverse_ref, in_ref = targets[count - 6 :]
    for copy in copies[: count - 3]:
        copy.wait()
    own_weights(targets[0], eye_ref, weight, work)
    pair_weights(targets[1 : count - 6], flip_ref, order_ref, weight, work, held, rows)
    for copy in copies[count - 3 :]:
        copy.wait()

    def weighted(values, v):
        part = weight[v]
        return (values * jnp.concatenate([part, part], axis=0)).astype(BF)

    def forward(rows, n):
        return dot_table(forward_ref, rows, n)

    def inverse(rows, n):
        return dot_table(inverse_ref, rows, n)

    loaded = [in_ref[:, w].reshape(256, 256) for w in range(6)]
    for e in range(2):
        total = None
        for s in range(3):
            rows = gather_groups([loaded[2 * r + e][:, 64 * s : 64 * (s + 1)] for r in range(3)])
            term = forward(rows, 1 + s)
            total = term if total is None else total + term
        spectrum = weighted(total, 6 + e)
        tails = [inverse(spectrum, 1 + s) for s in range(3)]
        for r in range(3):
            w = 2 * r + e
            values = inverse(weighted(forward(loaded[w], 0), w), 0)
            values = values + gather_groups([tail[:, 64 * r : 64 * (r + 1)] for tail in tails])
            out_ref[:, w] = values.astype(BF).reshape(16, 16, 256)


def third_kernel(in_ref, table_ref, out_ref, work):
    values = in_ref[...].astype(F32).reshape(1536, 256)
    work[0] = values[:, :128]
    work[1] = values[:, 128:]

    def inverse(rows, n):
        return dot(table_ref[0, n], rows) + dot(table_ref[1, n], rows)

    def load(row):
        return get_rows(work, row, 192).astype(BF)

    for e in range(2):
        rows = load(6 + e)
        tails = [inverse(rows, 1 + s) for s in range(3)]
        for r in range(3):
            t = 2 * r + e
            values = inverse(load(t), 0)
            values = values + gather_groups([tail[:, 64 * r : 64 * (r + 1)] for tail in tails])
            out_ref[:, t] = values.astype(BF).reshape(8, 16, 256)


def last_kernel(
    info_ref, in_ref, tb_ref, ta_ref, sign_ref, own_ref, send_ref, work, spare, both
):
    side = info_ref[2]
    values = in_ref[...].astype(F32).reshape(768, 256)
    work[0] = values[:, :128]
    work[1] = values[:, 128:]
    spare[...] = jnp.zeros_like(spare)
    for e in range(2):
        rows = get_rows(work, 6 + e, 96)
        spare[pl.ds(e, 96, stride=8), :] = rows[:, :128]
        spare[pl.ds(2 + e, 96, stride=8), :] = swap_half(rows[:, :128])
        spare[pl.ds(4 + e, 96, stride=8), :] = rows[:, 128:]
    low = low_half((48, 128))
    groups = [[] for _ in range(5)]
    shaped = values.reshape(8, 6, 2, 8, 256)
    shaped_spare = spare[...].reshape(8, 6, 2, 8, 128)
    for g in range(8):
        real_part = shaped[g, :, 0].reshape(48, 256)
        imag_part = shaped[g, :, 1].reshape(48, 256)
        for pair in range(2):
            real_tile = real_part[:, 128 * pair : 128 * (pair + 1)]
            imag_tile = imag_part[:, 128 * pair : 128 * (pair + 1)]
            groups[2 * pair].append(jnp.where(low, real_tile, swap_half(imag_tile)))
            groups[2 * pair + 1].append(jnp.where(low, swap_half(real_tile), imag_tile))
        real_tile = shaped_spare[g, :, 0].reshape(48, 128)
        imag_tile = shaped_spare[g, :, 1].reshape(48, 128)
        groups[4].append(jnp.where(low, real_tile, swap_half(imag_tile)))
    rows = jnp.concatenate([jnp.concatenate(group, axis=1) for group in groups], axis=0).astype(BF)
    half = dot_columns(rows, tb_ref).astype(BF)
    rows = jnp.concatenate(
        [
            jnp.concatenate(
                [half[48 * ig : 48 * (ig + 1), 128 * y : 128 * (y + 1)] for ig in range(5)], axis=1
            )
            for y in range(6)
        ],
        axis=0,
    )
    result = dot_columns(rows, ta_ref) * sign_ref[...]
    for y in range(6):
        both[y // 3, :, 384 * (y % 3) : 384 * (y % 3 + 1)] = result[48 * y : 48 * (y + 1)]
    own = both[side]
    for t in range(6):
        own_ref[t] = own[8 * t : 8 * t + 6]
    send_ref[...] = both[1 - side].astype(BF)


def sum_kernel(own_ref, other_ref, out_ref):
    other = other_ref[...].astype(F32)
    for t in range(6):
        out_ref[t] = own_ref[t] + other[8 * t : 8 * t + 6]


def device_of(a, z, c):
    return (a * 8 + (z // 2) * 2 + c) * 2 + z % 2


def column_pairs(shift, flip):
    return [
        (device_of(a, (z + shift) % 8, c ^ flip), device_of(a, z, c))
        for a in range(16)
        for z in range(8)
        for c in range(2)
    ]


def mirror_pairs(a_from, g_from):
    return [
        ((((a_from - a) % 16) * 8 + (g_from - g) % 8) * 2 + 1 - h, (a * 8 + g) * 2 + h)
        for a in range(16)
        for g in range(8)
        for h in range(2)
    ]


def gather_column(block):
    def receive(values, shift, flip=0):
        return lax.ppermute(values, AXES, column_pairs(shift, flip))

    held = {0: block}
    for shift in (1, 7, 2, 6):
        held[shift] = receive(block, shift)
    held[3] = receive(held[2], 1)
    held[5] = receive(held[6], 7)
    held[4] = receive(held[2], 2)
    blocks = []
    for shift in SHIFTS:
        blocks += [held[shift], receive(held[shift], 0, 1)]
    return blocks


def shape(dims, dtype):
    return jax.ShapeDtypeStruct(dims, dtype)


def body(current, kernel):
    g = lax.axis_index("gz")
    h = lax.axis_index("gy")
    info = jnp.stack([(g // 2) * 2 + h, g % 2, h, g]).astype(jnp.int32)
    parity = jnp.arange(384) % 2
    sign = jnp.where((parity == 1) & (h == 1), -1.0, 1.0).astype(F32)
    flip, order, eye = mirror_tables()

    anywhere = pl.BlockSpec(memory_space=pl.ANY)
    block = call(raw_kernel, shape((48, 1152), BF), [pltpu.VMEM((48, 1152), F32)], vmem=8)(current)
    blocks = gather_column(block)

    sent = call(
        weight_send_kernel,
        [shape((n, 48, 1152), BF) for n in PARTS]
        + [shape((48, 1152), BF), shape((24, 1152), BF), shape((8, 1152), BF)],
        [pltpu.VMEM((48, 1152), F32), pltpu.VMEM((32, 1152), F32)]
        + [pltpu.VMEM((6, 12, 4608), F32), pltpu.SemaphoreType.DMA],
        in_specs=[anywhere] * 17,
        vmem=59,
    )(kernel, *blocks)
    places = ((15, 7),) * len(PARTS) + ((16, 7), (15, 8), (16, 8))
    arrived = [lax.ppermute(s, AXES, mirror_pairs(*place)) for s, place in zip(sent, places)]
    def spread(*operands):
        values = call(
            forward_kernel,
            shape((16, 6, 16, 256), BF),
            [
                pltpu.VMEM((6, 8, 48, 384), BF),
                pltpu.VMEM((6, 384, 640), BF),
                pltpu.VMEM((2, 1536, 128), F32),
                pltpu.VMEM((16, 48, 1152), BF),
                pltpu.VMEM((1, 384, 640), BF),
                pltpu.VMEM((768, 256), BF),
                pltpu.VMEM((2, 192, 128), BF),
                pltpu.SemaphoreType.DMA((19,)),
            ],
            in_specs=[smem_spec(), vmem_spec()] + [anywhere] * 19,
            vmem=59,
        )(*operands)
        return lax.all_to_all(values, "ta", split_axis=0, concat_axis=0, tiled=True)

    values = lax.cond(
        g < lax.axis_size("gz"),
        spread,
        lambda *operands: jnp.zeros((16, 6, 16, 256), BF),
        info, sign[None, :], *blocks, jnp.asarray(first_forward()), jnp.asarray(second_forward()),
        jnp.asarray(third_forward()),
    )
    operands = (
        kernel, *arrived, jnp.asarray(eye), jnp.asarray(flip), jnp.asarray(order),
        jnp.asarray(time_forward()), jnp.asarray(time_inverse()), values
    )
    values = call(
        time_kernel,
        shape((16, 6, 16, 256), BF),
        [pltpu.VMEM((6, 12, 4864), F32)]
        + [pltpu.VMEM(operand.shape, operand.dtype) for operand in operands[1:]]
        + [
            pltpu.VMEM((8, 256, 192), F32),
            pltpu.VMEM((48, 1152), F32),
            pltpu.VMEM((32, 1152), F32),
            pltpu.VMEM((8, 192, 256), F32),
            pltpu.SemaphoreType.DMA((len(operands),)),
        ],
        in_specs=[anywhere] * len(operands),
        vmem=59,
    )(*operands)
    values = lax.all_to_all(values, "ta", split_axis=0, concat_axis=0, tiled=True)
    values = call(third_kernel, shape((8, 6, 16, 256), BF), [pltpu.VMEM((2, 1536, 128), F32)])(
        values, jnp.asarray(third_inverse())
    )
    values = lax.all_to_all(values, "gz", split_axis=0, concat_axis=0, tiled=True)
    own, send = call(
        last_kernel,
        [shape((6, 6, 1152), F32), shape((48, 1152), BF)],
        [
            pltpu.VMEM((2, 768, 128), F32),
            pltpu.VMEM((768, 128), F32),
            pltpu.VMEM((2, 48, 1152), F32),
        ],
        in_specs=[smem_spec()] + [vmem_spec()] * 4,
    )(info, values, jnp.asarray(second_inverse()), jnp.asarray(first_inverse()), sign[None, :])
    other = lax.ppermute(send, "gy", [(0, 1), (1, 0)])
    return call(sum_kernel, shape((6, 6, 1152), F32), vmem=8)(own, other)


def solution(mesh):
    specs = P("ta", "gz", "gy")
    return jax.shard_map(
        body, mesh=mesh, in_specs=(specs, specs), out_specs=specs, check_vma=False
    )
```
